32 devices in a mesh: tok: 16 (over z, y, x), head: 2 (over core).
Axes of the slice: x: 2, y: 2, z: 4, core: 2. Of those that a mesh axis runs over, the one named last changes fastest.
Arguments:
- queries: bfloat16 [2048, 1536], P('tok', 'head'), may hold values from -32 to 32
- keys: bfloat16 [2048, 1536], P('tok', 'head'), may hold values from -32 to 32
- values: bfloat16 [2048, 1536], P('tok', 'head'), may hold values from -6 to 6
- window: int32 [16, 27], P('tok'), may hold values from -1 to 15, as said below
- out_weight: bfloat16 [1536, 3072], P('head', 'tok'), may hold values from -0.15625 to 0.15625
Outputs:
- projected: bfloat16 [2048, 3072], P('tok', 'head')
The draws below stay inside these ranges and needn't reach their ends.
Inputs may be any that keep to these rules, and one draw needn't show every extreme that they name: `window`: row i lists distinct tiles: first i itself, then tiles whose frame, row and column each differ from those of i by at most one; -1 marks unused entries, which come last.
All inputs are finite; a program needn't handle non-finite values.
Results may differ from the reference program's by a relative error of at most 0.015.
Values may be sent and summed in bfloat16 or wider, within the bound.
A program may use at most 128 MiB of HBM per device.

```python
import jax
import jax.numpy as jnp
from jax import lax

D = 3072
HD = 128
HEAD_DEV = 6
TILE = 128
HEADS = 12
HH = 1536
TILES = 16
TW = 4
TH = 2
TF = 2
TOKENS = 2048
N_HEAD = 2


def draw_queries(key, part):
    key = jax.random.fold_in(key, 11)
    drawn = jax.random.normal(key, (TOKENS, HEADS * HD), jnp.float32)
    return drawn.astype(jnp.bfloat16)


def draw_keys(key, part):
    key = jax.random.fold_in(key, 12)
    drawn = jax.random.normal(key, (TOKENS, HEADS * HD), jnp.float32)
    return drawn.astype(jnp.bfloat16)


def draw_window(key, part):
    key = jax.random.fold_in(key, 5)
    frame_size = TW * TH
    tile_index = jnp.arange(TILES, dtype=jnp.int32)[:, None]
    column = jnp.arange(27, dtype=jnp.int32)[None, :]
    step_f = column // 9 - 1
    step_h = column // 3 % 3 - 1
    step_w = column % 3 - 1
    tile_frame = tile_index // frame_size
    tile_row = tile_index // TW % TH
    tile_col = tile_index % TW
    usable = (tile_frame + step_f >= 0) & (tile_frame + step_f < TF) & (tile_row + step_h >= 0) & (tile_row + step_h < TH) & (tile_col + step_w >= 0) & (tile_col + step_w < TW) & (column != 13)
    candidate = tile_index + step_f * frame_size + step_h * TW + step_w
    row_keys = jax.random.split(jax.random.fold_in(key, 1), TILES)
    shuffled = jax.vmap(lambda row_key: jax.random.permutation(row_key, 27))(row_keys).astype(jnp.int32)
    ranking = jnp.where(usable, shuffled, shuffled + 1000)
    order = jnp.argsort(ranking, axis=1)
    ordered = jnp.take_along_axis(candidate, order, axis=1)
    available = jnp.sum(usable.astype(jnp.int32), axis=1)
    wanted = jax.random.randint(jax.random.fold_in(key, 2), (TILES,), 8, 27)
    wanted = jnp.where(tile_index[:, 0] % 5 == 0, 26, wanted)
    listed_count = jnp.minimum(wanted, available)
    others = jnp.where(column < listed_count[:, None], ordered, -1)
    return jnp.concatenate([tile_index, others[:, :26]], axis=1).astype(jnp.int32)


def levels(rng, extent, cuts, smallest, largest):
    def one(position, blocks):
        heights = jax.random.uniform(jax.random.fold_in(jax.random.fold_in(rng, 6), position), (blocks,), jnp.float32, smallest / len(cuts), largest / len(cuts))
        return jnp.repeat(jnp.exp(heights), extent[position] // blocks).reshape((-1,) + (1,) * (len(extent) - position - 1))

    factor_of = one(*cuts[0])
    for cut in cuts[1:]:
        factor_of = factor_of * one(*cut)
    return factor_of


def scatter_about(rng, extent, spread, most, cuts=(), kind=jnp.bfloat16):
    array = spread * jax.random.normal(rng, extent, jnp.float32)
    if cuts:
        array = array * levels(rng, extent, cuts, -0.22, 0.18)
    return jnp.clip(array, -most, most).astype(kind)


def setup_inputs(seed: int = 0) -> dict:
    key_list = jax.random.split(jax.random.key(seed), 6)
    queries = draw_queries(jax.random.fold_in(key_list[5], 71), 0)
    keys = draw_keys(jax.random.fold_in(key_list[5], 71), 0)
    values = scatter_about(key_list[2], (TOKENS, HH), 1.0, 6.0, ((0, 16), (1, 2)))
    window = draw_window(jax.random.fold_in(key_list[5], 71), 0)
    out_weight = scatter_about(key_list[4], (HH, D), HH ** -0.5, 0.15625, ((0, 2), (1, 16)))
    return {"queries": queries, "keys": keys, "values": values, "window": window, "out_weight": out_weight}


def reference(queries, keys, values, window, out_weight):
    scale = HD ** -0.5
    query_tiles = queries.reshape(TILES, TILE, HEADS, HD)
    key_tiles = keys.reshape(TILES, TILE, HEADS, HD)
    value_tiles = values.reshape(TILES, TILE, HEADS, HD)

    def per_tile(tile_index):
        listed_tiles = window[tile_index]
        is_listed = listed_tiles >= 0
        safe_index = jnp.where(is_listed, listed_tiles, 0).astype(jnp.int32)
        chosen_keys = key_tiles[safe_index].astype(jnp.float32)
        chosen_values = value_tiles[safe_index].astype(jnp.float32)
        query_block = query_tiles[tile_index].astype(jnp.float32)
        scores = jnp.einsum("qhd,wkhd->hqwk", query_block, chosen_keys) * scale
        scores = jnp.where(is_listed[None, None, :, None], scores, -jnp.inf)
        peak = jnp.max(scores, axis=(2, 3), keepdims=True)
        unrounded = jnp.exp(scores - peak)
        total = jnp.sum(unrounded, axis=(2, 3))
        weights = lax.optimization_barrier(unrounded.astype(jnp.bfloat16)).astype(jnp.float32)
        summed = jnp.einsum("hqwk,wkhd->qhd", weights, chosen_values)
        return (summed / jnp.transpose(total)[:, :, None]).astype(jnp.bfloat16)

    attended = lax.map(per_tile, jnp.arange(TILES, dtype=jnp.int32)).reshape(TOKENS, HEADS * HD)
    group_width = HEAD_DEV * HD
    projected = jnp.zeros((TOKENS, D), jnp.float32)
    for head_group in range(N_HEAD):
        lower = head_group * group_width
        partial_sum = jnp.dot(attended[:, lower:lower + group_width], out_weight[lower:lower + group_width],
                              preferred_element_type=jnp.float32)
        projected = projected + lax.optimization_barrier(partial_sum.astype(jnp.bfloat16)).astype(jnp.float32)
    return projected.astype(jnp.bfloat16)
```

```python
import jax
import jax.numpy as jnp
from jax import lax
from jax.experimental import pallas as pl
from jax.experimental.pallas import tpu as pltpu
from jax.sharding import PartitionSpec as P

HD = 128
MESH = pl.DeviceIdType.MESH


def passed_along(value, axis, by):
    count = lax.axis_size(axis)
    pairs = [(i, i + by) for i in range(count) if 0 <= i + by < count]
    return lax.ppermute(value, axis, pairs)


def attend_tile(running, query_heads, kv_piece, is_listed):
    peak_now, total_now, summed_now = running
    tok_rows, head_count, head_size = query_heads.shape
    key_heads = kv_piece[0].reshape(tok_rows, head_count, head_size)
    value_heads = kv_piece[1].reshape(tok_rows, head_count, head_size)
    scores = jnp.einsum("qhd,khd->hqk", query_heads, key_heads, preferred_element_type=jnp.float32)
    scores = jnp.where(is_listed, scores * HD ** (-0.5), -1e30)
    new_peak = jnp.maximum(peak_now, jnp.max(scores, axis=-1))
    rescale = jnp.exp(peak_now - new_peak)
    unrounded = jnp.exp(scores - new_peak[..., None])
    total_next = total_now * rescale + jnp.sum(unrounded, axis=-1)
    weights = unrounded.astype(jnp.bfloat16)
    summed_next = summed_now * rescale[..., None] + jnp.einsum(
        "hqk,khd->hqd", weights, value_heads, preferred_element_type=jnp.float32
    )
    return (new_peak, total_next, summed_next)


def general_body(queries, keys, values, window, out_weight):
    tok_rows, feat_width = queries.shape
    head_count = feat_width // HD
    tile_count = lax.axis_size("tok")
    grid_w = min(8, tile_count // 4)
    grid_h = min(4, tile_count // (2 * grid_w))
    frame_size = grid_w * grid_h
    frame_count = tile_count // frame_size
    my_tile = lax.axis_index("tok")
    my_frame = my_tile // frame_size
    my_row = my_tile // grid_w % grid_h
    my_col = my_tile % grid_w
    query_heads = queries.reshape(tok_rows, head_count, HD)
    listed_tiles = window[0]
    initial = (
        jnp.full((head_count, tok_rows), -1e30, jnp.float32),
        jnp.zeros((head_count, tok_rows), jnp.float32),
        jnp.zeros((head_count, tok_rows, HD), jnp.float32),
    )
    own_pair = jnp.stack([keys, values])
    slot_blocks = []
    for step_f in (-1, 0, 1):
        for step_h in (-1, 0, 1):
            for step_w in (-1, 0, 1):
                distance = step_f * frame_size + step_h * grid_w + step_w
                if distance == 0:
                    slot_blocks.append(own_pair)
                else:
                    slot_blocks.append(passed_along(own_pair, "tok", -distance))
    near_box = jnp.stack(slot_blocks)
    slot_range = jnp.arange(27, dtype=jnp.int32)
    slot_f = slot_range // 9 - 1
    slot_h = slot_range // 3 % 3 - 1
    slot_w = slot_range % 3 - 1
    slot_distance = slot_f * frame_size + slot_h * grid_w + slot_w
    inside = (
        (my_frame + slot_f >= 0)
        & (my_frame + slot_f < frame_count)
        & (my_row + slot_h >= 0)
        & (my_row + slot_h < grid_h)
        & (my_col + slot_w >= 0)
        & (my_col + slot_w < grid_w)
    )

    def visit_band(running, slot_index):
        key_tile = my_tile + slot_distance[slot_index]
        is_listed = inside[slot_index] & jnp.any(listed_tiles == key_tile)
        kv_piece = lax.dynamic_index_in_dim(near_box, slot_index, 0, keepdims=False)
        return (attend_tile(running, query_heads, kv_piece, is_listed), None)

    running, _ = lax.scan(visit_band, initial, slot_range)
    attended = (running[2] / running[1][..., None]).transpose(1, 0, 2).reshape(tok_rows, feat_width)
    attended = attended.astype(jnp.bfloat16)
    projection = jnp.dot(
        attended,
        lax.all_gather(out_weight, "tok", axis=1, tiled=True),
        preferred_element_type=jnp.float32,
    )
    return lax.psum_scatter(
        projection.astype(jnp.bfloat16), "head", scatter_dimension=1, tiled=True
    )


def column_kernel(
    q_ref, k_ref, v_ref, win_ref, w_ref, o_ref,
    qbuf, bias_own, bias, kv, wbuf, wide, m_ref, l_ref, acc_ref, mine, att, part_out, part_in, staged,
    s_kv, s_q, s_b, s_w, s_fwd, s_sib, s_att, s_part, s_out,
    r_x, r_y, r_q, r_b, r_w, r_att, r_part, r_out,
):
    tile = lax.axis_index("tok")
    p = lax.axis_index("head")
    z = tile // 4
    c = tile % 4
    z_half = z // 2
    z_odd = z % 2
    xn = c + 1 - 2 * (c % 2)
    dn = 3 - c
    has_diag = (c == 1) | (c == 2)
    rows = q_ref.shape[0]
    span = q_ref.shape[1] // 2
    heads = span // HD
    cols = w_ref.shape[1]
    quarter = 4 * cols
    scale = HD ** (-0.5)

    def remote(src, dst, ssem, rsem, zt, ct, ht):
        return pltpu.make_async_remote_copy(
            src_ref=src, dst_ref=dst, send_sem=ssem, recv_sem=rsem,
            device_id=(zt * 4 + ct, ht), device_id_type=MESH,
        )

    sent = []

    def put(src, dst, ssem, rsem, zt, ct, ht):
        here = (zt == z) & (ht == p)

        @pl.when(here)
        def _():
            pltpu.make_async_copy(src, dst, rsem).start()

        @pl.when(jnp.logical_not(here))
        def _():
            remote(src, dst, ssem, rsem, zt, ct, ht).start()

        sent.append((jnp.logical_not(here), remote(src, dst, ssem, rsem, zt, ct, ht)))

    def arrived(dst, rsem):
        pltpu.make_async_copy(dst, dst, rsem).wait()

    barrier = pltpu.get_barrier_semaphore()
    for k in range(1, 4):
        for h in range(2):
            pl.semaphore_signal(barrier, inc=1, device_id=((z + k) % 4 * 4 + c, h), device_id_type=MESH)
        pl.semaphore_signal(barrier, inc=1, device_id=(z * 4 + (c + k) % 4, p), device_id_type=MESH)
    pl.semaphore_signal(barrier, inc=1, device_id=(tile, 1 - p), device_id_type=MESH)

    row = lax.broadcasted_iota(jnp.int32, (16, win_ref.shape[1]), 0)
    slot = row // 4
    column = jnp.where(slot == 0, c, jnp.where(slot == 1, xn, dn))
    key_tile = row % 4 * 4 + column
    listed = jnp.where(win_ref[...] == key_tile, 0.0, -1e30)
    bias_own[...] = jnp.broadcast_to(jnp.max(listed, axis=1, keepdims=True), bias_own.shape)

    pl.semaphore_wait(barrier, 10)

    for i in range(2):
        zd = 2 * p + i
        part = slice(i * span, (i + 1) * span)
        put(k_ref.at[:, part], kv.at[0, 0, z], s_kv.at[i, 0], r_x.at[0, z], zd, c, 0)
        put(v_ref.at[:, part], kv.at[1, 0, z], s_kv.at[i, 1], r_x.at[0, z], zd, c, 1)
    for i in range(2):
        zd = 2 * p + i
        part = slice(i * span, (i + 1) * span)
        put(q_ref.at[:, part], qbuf.at[z_odd], s_q.at[i], r_q.at[z_odd], zd, c, z_half)
        put(bias_own, bias.at[z_odd], s_b.at[i], r_b.at[z_odd], zd, c, z_half)
    weight_copies = []
    for k in range(1, 4):
        copy = remote(w_ref, wbuf.at[c], s_w.at[k], r_w.at[c], z, (c + k) % 4, p)
        copy.start()
        weight_copies.append(copy)
    own_weight = pltpu.make_async_copy(w_ref, wbuf.at[c], r_w.at[c])
    own_weight.start()

    plane, diagonal, siblings = [], [], []
    for k in range(4):
        zz = (z + k) % 4
        piece = kv.at[p, 0, zz]
        arrived(piece, r_x.at[0, zz])
        copy = remote(piece, kv.at[p, 1, zz], s_fwd.at[0, k], r_x.at[1, zz], z, xn, p)
        copy.start()
        plane.append(copy)
        copy = remote(piece, kv.at[p, 2, zz], s_fwd.at[1, k], r_x.at[2, zz], z, dn, p)
        pl.when(has_diag)(copy.start)
        diagonal.append(copy)
        copy = remote(piece, piece, s_sib.at[0, k], r_y.at[0, zz], z, c, 1 - p)
        copy.start()
        siblings.append(copy)

    def share(s):
        copies = []
        for k in range(4):
            zz = (z + k) % 4
            piece = kv.at[p, s, zz]
            arrived(piece, r_x.at[s, zz])
            copy = remote(piece, piece, s_sib.at[s, k], r_y.at[s, zz], z, c, 1 - p)
            copy.start()
            copies.append(copy)
        return copies

    def collect(s):
        for zz in range(4):
            arrived(kv.at[1 - p, s, zz], r_y.at[s, zz])

    def attend(s):
        for j in range(heads):
            lanes = slice(j * HD, (j + 1) * HD)
            k_all = kv[0, s, :, :, lanes].reshape(4 * rows, HD)
            v_all = kv[1, s, :, :, lanes].reshape(4 * rows, HD)
            for i in range(2):
                n = j * 2 + i
                scores = lax.dot_general(
                    qbuf[i, :, lanes], k_all, (((1,), (1,)), ((), ())), preferred_element_type=jnp.float32
                )
                shift = jnp.concatenate([bias[i, s * 4 + t:s * 4 + t + 1, :] for t in range(4)], axis=1)
                scores = scores * scale + shift
                top = jnp.max(scores, axis=1, keepdims=True)
                if s == 0:
                    peak = top
                else:
                    before = m_ref[n][:, :1]
                    peak = jnp.maximum(before, top)
                    rescale = jnp.exp(before - peak)
                unrounded = jnp.exp(scores - peak)
                total = jnp.sum(unrounded, axis=1, keepdims=True)
                summed = jnp.dot(unrounded.astype(jnp.bfloat16), v_all, preferred_element_type=jnp.float32)
                if s > 0:
                    total = total + l_ref[n][:, :1] * rescale
                    summed = summed + acc_ref[n] * rescale
                m_ref[n] = jnp.broadcast_to(peak, (rows, HD))
                l_ref[n] = jnp.broadcast_to(total, (rows, HD))
                acc_ref[n] = summed

    for i in range(2):
        arrived(qbuf.at[i], r_q.at[i])
        arrived(bias.at[i], r_b.at[i])
    collect(0)
    attend(0)
    siblings += share(1)
    collect(1)
    attend(1)

    @pl.when(has_diag)
    def _():
        copies = share(2)
        collect(2)
        attend(2)
        for copy in copies:
            copy.wait_send()

    for j in range(heads):
        for i in range(2):
            n = j * 2 + i
            mine[i * rows:(i + 1) * rows, j * HD:(j + 1) * HD] = (acc_ref[n] / l_ref[n]).astype(jnp.bfloat16)

    for k in range(4):
        put(mine, att.at[z_odd, p], s_att.at[k], r_att.at[z_odd, p], (z + k) % 4, c, z_half)

    for cc in range(4):
        arrived(wbuf.at[cc], r_w.at[cc])
        wide[:, cc * cols:(cc + 1) * cols] = wbuf[cc]

    for zf in range(2):
        for pp in range(2):
            arrived(att.at[zf, pp], r_att.at[zf, pp])

    def project(half):
        return jnp.dot(att[0, half], wide[:span, :], preferred_element_type=jnp.float32) + jnp.dot(
            att[1, half], wide[span:, :], preferred_element_type=jnp.float32
        )

    part_out[...] = project(1 - p).astype(jnp.bfloat16)
    swap = remote(part_out, part_in, s_part, r_part, z, c, 1 - p)
    swap.start()
    own = project(p).astype(jnp.bfloat16).astype(jnp.float32)
    swap.wait_recv()
    staged[...] = (own + part_in[...].astype(jnp.float32)).astype(jnp.bfloat16)

    place = pl.ds(pl.multiple_of(z_odd * quarter, quarter), quarter)
    for i in range(2):
        put(staged.at[i * rows:(i + 1) * rows, :], o_ref.at[:, place], s_out.at[i], r_out.at[z_odd], 2 * p + i, c, z_half)
    for zf in range(2):
        arrived(o_ref.at[:, zf * quarter:(zf + 1) * quarter], r_out.at[zf])

    swap.wait_send()
    for copy in weight_copies + plane + siblings:
        copy.wait_send()

    @pl.when(has_diag)
    def _():
        for copy in diagonal:
            copy.wait_send()

    for away, copy in sent:
        pl.when(away)(copy.wait_send)


def column_body(queries, keys, values, window, out_weight):
    rows, width = queries.shape
    depth, cols = out_weight.shape
    span = width // 2
    states = 2 * (span // HD)
    bf16, f32 = jnp.bfloat16, jnp.float32
    dma = pltpu.SemaphoreType.DMA
    vmem = pl.BlockSpec(memory_space=pltpu.VMEM)
    return pl.pallas_call(
        column_kernel,
        out_shape=jax.ShapeDtypeStruct((rows, 8 * cols), bf16),
        in_specs=[vmem] * 5,
        out_specs=vmem,
        scratch_shapes=[
            pltpu.VMEM((2, rows, span), bf16),
            pltpu.VMEM((16, 128), f32),
            pltpu.VMEM((2, 16, 128), f32),
            pltpu.VMEM((2, 3, 4, rows, span), bf16),
            pltpu.VMEM((4, depth, cols), bf16),
            pltpu.VMEM((depth, 4 * cols), bf16),
            pltpu.VMEM((states, rows, HD), f32),
            pltpu.VMEM((states, rows, HD), f32),
            pltpu.VMEM((states, rows, HD), f32),
            pltpu.VMEM((2 * rows, span), bf16),
            pltpu.VMEM((2, 2, 2 * rows, span), bf16),
            pltpu.VMEM((2 * rows, 4 * cols), bf16),
            pltpu.VMEM((2 * rows, 4 * cols), bf16),
            pltpu.VMEM((2 * rows, 4 * cols), bf16),
            dma((2, 2)), dma((2,)), dma((2,)), dma((4,)), dma((2, 4)), dma((3, 4)), dma((4,)), dma, dma((2,)),
            dma((3, 4)), dma((3, 4)), dma((2,)), dma((2,)), dma((4,)), dma((2, 2)), dma, dma((2,)),
        ],
        compiler_params=pltpu.CompilerParams(
            collective_id=0, has_side_effects=True, vmem_limit_bytes=48 * 1024 * 1024
        ),
        cost_estimate=pl.CostEstimate(flops=1300000000, bytes_accessed=3000000, transcendentals=1200000),
    )(queries, keys, values, window, out_weight)


def solution(mesh):
    in_specs = (
        P("tok", "head"),
        P("tok", "head"),
        P("tok", "head"),
        P("tok", None),
        P("head", "tok"),
    )
    out_specs = P("tok", "head")
    small_grid = mesh.shape["tok"] == 16 and mesh.shape["head"] == 2
    body = column_body if small_grid else general_body
    return jax.shard_map(body, mesh=mesh, in_specs=in_specs, out_specs=out_specs, check_vma=False)
```

```python
import jax
import jax.numpy as jnp
from jax import lax
from jax.experimental import pallas as pl
from jax.experimental.pallas import tpu as pltpu
from jax.sharding import PartitionSpec as P

HD = 128
MESH = pl.DeviceIdType.MESH


def passed_along(value, axis, by):
    count = lax.axis_size(axis)
    pairs = [(i, i + by) for i in range(count) if 0 <= i + by < count]
    return lax.ppermute(value, axis, pairs)


def attend_tile(running, query_heads, kv_piece, is_listed):
    peak_now, total_now, summed_now = running
    tok_rows, head_count, head_size = query_heads.shape
    key_heads = kv_piece[0].reshape(tok_rows, head_count, head_size)
    value_heads = kv_piece[1].reshape(tok_rows, head_count, head_size)
    scores = jnp.einsum("qhd,khd->hqk", query_heads, key_heads, preferred_element_type=jnp.float32)
    scores = jnp.where(is_listed, scores * HD ** (-0.5), -1e30)
    new_peak = jnp.maximum(peak_now, jnp.max(scores, axis=-1))
    rescale = jnp.exp(peak_now - new_peak)
    unrounded = jnp.exp(scores - new_peak[..., None])
    total_next = total_now * rescale + jnp.sum(unrounded, axis=-1)
    weights = unrounded.astype(jnp.bfloat16)
    summed_next = summed_now * rescale[..., None] + jnp.einsum(
        "hqk,khd->hqd", weights, value_heads, preferred_element_type=jnp.float32
    )
    return (new_peak, total_next, summed_next)


def general_body(queries, keys, values, window, out_weight):
    tok_rows, feat_width = queries.shape
    head_count = feat_width // HD
    tile_count = lax.axis_size("tok")
    grid_w = min(8, tile_count // 4)
    grid_h = min(4, tile_count // (2 * grid_w))
    frame_size = grid_w * grid_h
    frame_count = tile_count // frame_size
    my_tile = lax.axis_index("tok")
    my_frame = my_tile // frame_size
    my_row = my_tile // grid_w % grid_h
    my_col = my_tile % grid_w
    query_heads = queries.reshape(tok_rows, head_count, HD)
    listed_tiles = window[0]
    initial = (
        jnp.full((head_count, tok_rows), -1e30, jnp.float32),
        jnp.zeros((head_count, tok_rows), jnp.float32),
        jnp.zeros((head_count, tok_rows, HD), jnp.float32),
    )
    own_pair = jnp.stack([keys, values])
    slot_blocks = []
    for step_f in (-1, 0, 1):
        for step_h in (-1, 0, 1):
            for step_w in (-1, 0, 1):
                distance = step_f * frame_size + step_h * grid_w + step_w
                if distance == 0:
                    slot_blocks.append(own_pair)
                else:
                    slot_blocks.append(passed_along(own_pair, "tok", -distance))
    near_box = jnp.stack(slot_blocks)
    slot_range = jnp.arange(27, dtype=jnp.int32)
    slot_f = slot_range // 9 - 1
    slot_h = slot_range // 3 % 3 - 1
    slot_w = slot_range % 3 - 1
    slot_distance = slot_f * frame_size + slot_h * grid_w + slot_w
    inside = (
        (my_frame + slot_f >= 0)
        & (my_frame + slot_f < frame_count)
        & (my_row + slot_h >= 0)
        & (my_row + slot_h < grid_h)
        & (my_col + slot_w >= 0)
        & (my_col + slot_w < grid_w)
    )

    def visit_band(running, slot_index):
        key_tile = my_tile + slot_distance[slot_index]
        is_listed = inside[slot_index] & jnp.any(listed_tiles == key_tile)
        kv_piece = lax.dynamic_index_in_dim(near_box, slot_index, 0, keepdims=False)
        return (attend_tile(running, query_heads, kv_piece, is_listed), None)

    running, _ = lax.scan(visit_band, initial, slot_range)
    attended = (running[2] / running[1][..., None]).transpose(1, 0, 2).reshape(tok_rows, feat_width)
    attended = attended.astype(jnp.bfloat16)
    projection = jnp.dot(
        attended,
        lax.all_gather(out_weight, "tok", axis=1, tiled=True),
        preferred_element_type=jnp.float32,
    )
    return lax.psum_scatter(
        projection.astype(jnp.bfloat16), "head", scatter_dimension=1, tiled=True
    )


def column_kernel(
    q_ref, k_ref, v_ref, win_ref, w_ref, o_ref,
    qbuf, bias_own, bias, kv, wide, mine, att, part_out, part_in, staged,
    send, r_x, r_y, r_q, r_b, r_w, r_att, r_part, r_out,
):
    tile = lax.axis_index("tok")
    p = lax.axis_index("head")
    z = tile // 4
    c = tile % 4
    z_half = z // 2
    z_odd = z % 2
    xn = c + 1 - 2 * (c % 2)
    yn = (c + 2) % 4
    dn = 3 - c
    inner = (c == 1) | (c == 2)
    outer = jnp.logical_not(inner)
    rows = q_ref.shape[0]
    span = q_ref.shape[1] // 2
    heads = span // HD
    quarter = 4 * w_ref.shape[0]
    scale = HD ** (-0.5)

    sent = []

    def remote(src, dst, rsem, zt, ct, ht):
        return pltpu.make_async_remote_copy(
            src_ref=src, dst_ref=dst, send_sem=send.at[len(sent)], recv_sem=rsem,
            device_id=(zt * 4 + ct, ht), device_id_type=MESH,
        )

    def push(src, dst, rsem, zt, ct, ht, when=None):
        copy = remote(src, dst, rsem, zt, ct, ht)
        if when is None:
            copy.start()
        else:
            pl.when(when)(copy.start)
        sent.append((when, copy))

    def put(src, dst, rsem, zt, ct, ht):
        here = (zt == z) & (ht == p)

        @pl.when(here)
        def _():
            pltpu.make_async_copy(src, dst, rsem).start()

        push(src, dst, rsem, zt, ct, ht, jnp.logical_not(here))

    def arrived(dst, rsem):
        pltpu.make_async_copy(dst, dst, rsem).wait()

    def lanes_of(j, base=0):
        return slice(base + j * HD, base + (j + 1) * HD)

    barrier = pltpu.get_barrier_semaphore()
    for k in range(1, 4):
        for h in range(2):
            pl.semaphore_signal(barrier, inc=1, device_id=((z + k) % 4 * 4 + c, h), device_id_type=MESH)
    for ct in (xn, yn):
        pl.semaphore_signal(barrier, inc=1, device_id=(z * 4 + ct, p), device_id_type=MESH)
    pl.semaphore_signal(barrier, inc=1, device_id=(tile, 1 - p), device_id_type=MESH)

    row = lax.broadcasted_iota(jnp.int32, (16, win_ref.shape[1]), 0)
    slot = row // 4
    column = jnp.where(slot == 0, c, jnp.where(slot == 1, xn, dn))
    key_tile = row % 4 * 4 + column
    listed = jnp.where(win_ref[...] == key_tile, 0.0, -1e30)
    bias_own[...] = jnp.broadcast_to(jnp.max(listed, axis=1, keepdims=True), bias_own.shape)

    pl.semaphore_wait(barrier, 9)

    for j in range(heads):
        for i in range(2):
            zd = 2 * p + i
            here, there = lanes_of(j, i * span), lanes_of(j)
            put(k_ref.at[:, here], kv.at[0, 0, z, :, there], r_x.at[0, j, z], zd, c, 0)
            put(v_ref.at[:, here], kv.at[1, 0, z, :, there], r_x.at[0, j, z], zd, c, 1)
            put(q_ref.at[:, here], qbuf.at[z_odd, :, there], r_q.at[j, z_odd], zd, c, z_half)
            if j == 0:
                put(bias_own, bias.at[z_odd], r_b.at[z_odd], zd, c, z_half)
        if j == 0:
            for ct in (xn, yn):
                push(w_ref, wide.at[c], r_w.at[c], z, ct, p)
            pltpu.make_async_copy(w_ref, wide.at[c], r_w.at[c]).start()

    def spread(j):
        there = lanes_of(j)
        for k in range(4):
            zz = (z + k) % 4
            piece = kv.at[p, 0, zz, :, there]
            arrived(piece, r_x.at[0, j, zz])
            push(piece, kv.at[p, 1, zz, :, there], r_x.at[1, j, zz], z, xn, p)
            push(piece, piece, r_y.at[0, j, zz], z, c, 1 - p)
        for k in range(4):
            zz = (z + k) % 4
            piece = kv.at[p, 1, zz, :, there]
            arrived(piece, r_x.at[1, j, zz])
            push(piece, kv.at[p, 2, zz, :, there], r_x.at[2, j, zz], z, yn, p, outer)
            push(piece, piece, r_y.at[1, j, zz], z, c, 1 - p)
        for k in range(4):
            zz = (z + k) % 4
            piece = kv.at[p, 2, zz, :, there]

            @pl.when(inner)
            def _():
                arrived(piece, r_x.at[2, j, zz])

            push(piece, piece, r_y.at[2, j, zz], z, c, 1 - p, inner)

    def attend_slots(j, slots):
        there = lanes_of(j)
        for s in range(slots):
            for zz in range(4):
                arrived(kv.at[1 - p, s, zz, :, there], r_y.at[s, j, zz])
        k_all = kv[0, :slots, :, :, there].reshape(slots * 4 * rows, HD)
        v_all = kv[1, :slots, :, :, there].reshape(slots * 4 * rows, HD)
        for i in range(2):
            scores = lax.dot_general(
                qbuf[i, :, there], k_all, (((1,), (1,)), ((), ())), preferred_element_type=jnp.float32
            )
            shift = jnp.concatenate([bias[i, t:t + 1, :] for t in range(slots * 4)], axis=1)
            scores = scores * scale + shift
            peak = jnp.max(scores, axis=1, keepdims=True)
            unrounded = jnp.exp(scores - peak)
            total = jnp.sum(unrounded, axis=1, keepdims=True)
            summed = jnp.dot(unrounded.astype(jnp.bfloat16), v_all, preferred_element_type=jnp.float32)
            mine[i * rows:(i + 1) * rows, there] = (summed / total).astype(jnp.bfloat16)

    def attend(j):
        for i in range(2):
            arrived(qbuf.at[i, :, lanes_of(j)], r_q.at[j, i])
            if j == 0:
                arrived(bias.at[i], r_b.at[i])
        pl.when(inner)(lambda: attend_slots(j, 3))
        pl.when(outer)(lambda: attend_slots(j, 2))
        there = lanes_of(j)
        put(mine.at[:, there], att.at[z_odd, p, :, there], r_att.at[z_odd, p, j], z, c, z_half)

    near = jnp.where(z > 2 * p, 1, 0)

    def carry(j):
        there = lanes_of(j)
        for zf in (near, 1 - near):
            origin = 2 * p + zf
            for half in range(2):
                piece = att.at[zf, half, :, there]
                arrived(piece, r_att.at[zf, half, j])
                push(piece, piece, r_att.at[zf, half, j], (z + 1) % 4, c, p, (origin <= z) & (z < 3))
                push(piece, piece, r_att.at[zf, half, j], (z + 3) % 4, c, p, (origin >= z) & (z > 0))

    spread(0)
    spread(1)
    for ct in (xn, yn):
        arrived(wide.at[ct], r_w.at[ct])
    passed = jnp.where(inner, xn, yn)
    push(wide.at[passed], wide.at[passed], r_w.at[passed], z, jnp.where(inner, yn, xn), p)
    attend(0)
    spread(2)
    attend(1)
    carry(0)
    attend(2)
    carry(1)
    carry(2)

    arrived(wide.at[c], r_w.at[c])
    arrived(wide.at[dn], r_w.at[dn])

    def project(half):
        sums = [
            lax.dot_general(
                att[zf, half], wide[:, :, zf * span:(zf + 1) * span].reshape(quarter, span),
                (((1,), (1,)), ((), ())), preferred_element_type=jnp.float32,
            )
            for zf in range(2)
        ]
        return (sums[0] + sums[1]).astype(jnp.bfloat16)

    part_out[...] = project(1 - p)
    push(part_out, part_in, r_part, z, c, 1 - p)
    own = project(p).astype(jnp.float32)
    arrived(part_in, r_part)
    staged[...] = (own + part_in[...].astype(jnp.float32)).astype(jnp.bfloat16)

    place = pl.ds(pl.multiple_of(z_odd * quarter, quarter), quarter)
    for i in range(2):
        put(staged.at[i * rows:(i + 1) * rows, :], o_ref.at[:, place], r_out.at[z_odd], 2 * p + i, c, z_half)
    for zf in range(2):
        arrived(o_ref.at[:, zf * quarter:(zf + 1) * quarter], r_out.at[zf])

    for when, copy in sent:
        if when is None:
            copy.wait_send()
        else:
            pl.when(when)(copy.wait_send)


def column_body(queries, keys, values, window, out_weight):
    rows, width = queries.shape
    depth, cols = out_weight.shape
    span = width // 2
    heads = span // HD
    bf16, f32 = jnp.bfloat16, jnp.float32
    dma = pltpu.SemaphoreType.DMA
    vmem = pl.BlockSpec(memory_space=pltpu.VMEM)
    copies = heads * (6 + 20 + 1 + 8) + 2 + 3 + 1 + 2
    return pl.pallas_call(
        column_kernel,
        out_shape=jax.ShapeDtypeStruct((rows, 8 * cols), bf16),
        in_specs=[vmem] * 5,
        out_specs=vmem,
        scratch_shapes=[
            pltpu.VMEM((2, rows, span), bf16),
            pltpu.VMEM((16, 128), f32),
            pltpu.VMEM((2, 16, 128), f32),
            pltpu.VMEM((2, 3, 4, rows, span), bf16),
            pltpu.VMEM((4, cols, depth), bf16),
            pltpu.VMEM((2 * rows, span), bf16),
            pltpu.VMEM((2, 2, 2 * rows, span), bf16),
            pltpu.VMEM((2 * rows, 4 * cols), bf16),
            pltpu.VMEM((2 * rows, 4 * cols), bf16),
            pltpu.VMEM((2 * rows, 4 * cols), bf16),
            dma((copies,)),
            dma((3, heads, 4)), dma((3, heads, 4)), dma((heads, 2)), dma((2,)), dma((4,)), dma((2, 2, heads)), dma, dma((2,)),
        ],
        compiler_params=pltpu.CompilerParams(
            collective_id=0, has_side_effects=True, vmem_limit_bytes=48 * 1024 * 1024
        ),
        cost_estimate=pl.CostEstimate(flops=1300000000, bytes_accessed=3000000, transcendentals=1200000),
    )(queries, keys, values, window, out_weight.T)


def solution(mesh):
    in_specs = (
        P("tok", "head"),
        P("tok", "head"),
        P("tok", "head"),
        P("tok", None),
        P("head", "tok"),
    )
    out_specs = P("tok", "head")
    small_grid = mesh.shape["tok"] == 16 and mesh.shape["head"] == 2
    body = column_body if small_grid else general_body
    return jax.shard_map(body, mesh=mesh, in_specs=in_specs, out_specs=out_specs, check_vma=False)
```

```python
import jax
import jax.numpy as jnp
from jax import lax
from jax.experimental import pallas as pl
from jax.experimental.pallas import tpu as pltpu
from jax.sharding import PartitionSpec as P

HD = 128
MESH = pl.DeviceIdType.MESH


def passed_along(value, axis, by):
    count = lax.axis_size(axis)
    pairs = [(i, i + by) for i in range(count) if 0 <= i + by < count]
    return lax.ppermute(value, axis, pairs)


def attend_tile(running, query_heads, kv_piece, is_listed):
    peak_now, total_now, summed_now = running
    tok_rows, head_count, head_size = query_heads.shape
    key_heads = kv_piece[0].reshape(tok_rows, head_count, head_size)
    value_heads = kv_piece[1].reshape(tok_rows, head_count, head_size)
    scores = jnp.einsum("qhd,khd->hqk", query_heads, key_heads, preferred_element_type=jnp.float32)
    scores = jnp.where(is_listed, scores * HD ** (-0.5), -1e30)
    new_peak = jnp.maximum(peak_now, jnp.max(scores, axis=-1))
    rescale = jnp.exp(peak_now - new_peak)
    unrounded = jnp.exp(scores - new_peak[..., None])
    total_next = total_now * rescale + jnp.sum(unrounded, axis=-1)
    weights = unrounded.astype(jnp.bfloat16)
    summed_next = summed_now * rescale[..., None] + jnp.einsum(
        "hqk,khd->hqd", weights, value_heads, preferred_element_type=jnp.float32
    )
    return (new_peak, total_next, summed_next)


def general_body(queries, keys, values, window, out_weight):
    tok_rows, feat_width = queries.shape
    head_count = feat_width // HD
    tile_count = lax.axis_size("tok")
    grid_w = min(8, tile_count // 4)
    grid_h = min(4, tile_count // (2 * grid_w))
    frame_size = grid_w * grid_h
    frame_count = tile_count // frame_size
    my_tile = lax.axis_index("tok")
    my_frame = my_tile // frame_size
    my_row = my_tile // grid_w % grid_h
    my_col = my_tile % grid_w
    query_heads = queries.reshape(tok_rows, head_count, HD)
    listed_tiles = window[0]
    initial = (
        jnp.full((head_count, tok_rows), -1e30, jnp.float32),
        jnp.zeros((head_count, tok_rows), jnp.float32),
        jnp.zeros((head_count, tok_rows, HD), jnp.float32),
    )
    own_pair = jnp.stack([keys, values])
    slot_blocks = []
    for step_f in (-1, 0, 1):
        for step_h in (-1, 0, 1):
            for step_w in (-1, 0, 1):
                distance = step_f * frame_size + step_h * grid_w + step_w
                if distance == 0:
                    slot_blocks.append(own_pair)
                else:
                    slot_blocks.append(passed_along(own_pair, "tok", -distance))
    near_box = jnp.stack(slot_blocks)
    slot_range = jnp.arange(27, dtype=jnp.int32)
    slot_f = slot_range // 9 - 1
    slot_h = slot_range // 3 % 3 - 1
    slot_w = slot_range % 3 - 1
    slot_distance = slot_f * frame_size + slot_h * grid_w + slot_w
    inside = (
        (my_frame + slot_f >= 0)
        & (my_frame + slot_f < frame_count)
        & (my_row + slot_h >= 0)
        & (my_row + slot_h < grid_h)
        & (my_col + slot_w >= 0)
        & (my_col + slot_w < grid_w)
    )

    def visit_band(running, slot_index):
        key_tile = my_tile + slot_distance[slot_index]
        is_listed = inside[slot_index] & jnp.any(listed_tiles == key_tile)
        kv_piece = lax.dynamic_index_in_dim(near_box, slot_index, 0, keepdims=False)
        return (attend_tile(running, query_heads, kv_piece, is_listed), None)

    running, _ = lax.scan(visit_band, initial, slot_range)
    attended = (running[2] / running[1][..., None]).transpose(1, 0, 2).reshape(tok_rows, feat_width)
    attended = attended.astype(jnp.bfloat16)
    projection = jnp.dot(
        attended,
        lax.all_gather(out_weight, "tok", axis=1, tiled=True),
        preferred_element_type=jnp.float32,
    )
    return lax.psum_scatter(
        projection.astype(jnp.bfloat16), "head", scatter_dimension=1, tiled=True
    )


def column_kernel(
    q_ref, k_ref, v_ref, win_ref, w_ref, o_ref,
    listing, qbuf, bias_own, bias, kv, wide, mine, att, part_out, part_in, staged,
    send, s_win, r_x, r_plane, r_y, r_q, r_b, r_w, r_att, r_part, r_out,
):
    tile = lax.axis_index("tok")
    p = lax.axis_index("head")
    z = tile // 4
    c = tile % 4
    z_half = z // 2
    z_odd = z % 2
    xn = c + 1 - 2 * (c % 2)
    yn = (c + 2) % 4
    dn = 3 - c
    inner = (c == 1) | (c == 2)
    outer = jnp.logical_not(inner)
    rows = q_ref.shape[0]
    span = q_ref.shape[1] // 2
    heads = span // HD
    quarter = 4 * w_ref.shape[0]
    scale = HD ** (-0.5)

    sent = []

    def remote(src, dst, rsem, zt, ct, ht):
        return pltpu.make_async_remote_copy(
            src_ref=src, dst_ref=dst, send_sem=send.at[len(sent)], recv_sem=rsem,
            device_id=(zt * 4 + ct, ht), device_id_type=MESH,
        )

    def push(src, dst, rsem, zt, ct, ht, when=None):
        copy = remote(src, dst, rsem, zt, ct, ht)
        if when is None:
            copy.start()
        else:
            pl.when(when)(copy.start)
        sent.append((when, copy))

    def put(src, dst, rsem, zt, ct, ht):
        here = (zt == z) & (ht == p)

        @pl.when(here)
        def _():
            pltpu.make_async_copy(src, dst, rsem).start()

        push(src, dst, rsem, zt, ct, ht, jnp.logical_not(here))

    def arrived(dst, rsem):
        pltpu.make_async_copy(dst, dst, rsem).wait()

    def lanes_of(j, base=0):
        return slice(base + j * HD, base + (j + 1) * HD)

    window_copy = pltpu.make_async_copy(win_ref, listing, s_win)
    window_copy.start()
    barrier = pltpu.get_barrier_semaphore()
    for k in range(1, 4):
        for h in range(2):
            pl.semaphore_signal(barrier, inc=1, device_id=((z + k) % 4 * 4 + c, h), device_id_type=MESH)
    for ct in (xn, yn):
        pl.semaphore_signal(barrier, inc=1, device_id=(z * 4 + ct, p), device_id_type=MESH)
    pl.semaphore_signal(barrier, inc=1, device_id=(tile, 1 - p), device_id_type=MESH)

    window_copy.wait()
    row = lax.broadcasted_iota(jnp.int32, (16, win_ref.shape[1]), 0)
    slot = row // 4
    column = jnp.where(slot == 0, c, jnp.where(slot == 1, xn, dn))
    key_tile = row % 4 * 4 + column
    listed = jnp.where(listing[...] == key_tile, 0.0, -1e30)
    bias_own[...] = jnp.broadcast_to(jnp.max(listed, axis=1, keepdims=True), bias_own.shape)

    pl.semaphore_wait(barrier, 9)

    for j in range(heads):
        for i in range(2):
            zd = 2 * p + i
            here = lanes_of(j, i * span)
            put(k_ref.at[:, here], kv.at[0, 0, j, z], r_x.at[j, z], zd, c, 0)
            put(v_ref.at[:, here], kv.at[1, 0, j, z], r_x.at[j, z], zd, c, 1)
            put(q_ref.at[:, here], qbuf.at[j, z_odd], r_q.at[j, z_odd], zd, c, z_half)
            if j == 0:
                put(bias_own, bias.at[z_odd], r_b.at[z_odd], zd, c, z_half)
        if j == 0:
            for ct in (xn, yn):
                push(w_ref, wide.at[c], r_w.at[c], z, ct, p)
            pltpu.make_async_copy(w_ref, wide.at[c], r_w.at[c]).start()

    def share(s, j, when=None):
        push(kv.at[p, s, j], kv.at[p, s, j], r_y.at[s, j], z, c, 1 - p, when)

    def spread_own(j):
        for k in range(4):
            zz = (z + k) % 4
            piece = kv.at[p, 0, j, zz]
            arrived(piece, r_x.at[j, zz])
            push(piece, kv.at[p, 1, j, zz], r_plane.at[0, j], z, xn, p)
        share(0, j)

    def spread_beside(j):
        piece = kv.at[p, 1, j]
        arrived(piece, r_plane.at[0, j])
        push(piece, kv.at[p, 2, j], r_plane.at[1, j], z, yn, p, outer)
        share(1, j)

    def spread_diagonal(j):
        pl.when(inner)(lambda: arrived(kv.at[p, 2, j], r_plane.at[1, j]))
        share(2, j, inner)

    def attend_slots(j, slots):
        for s in range(slots):
            arrived(kv.at[1 - p, s, j], r_y.at[s, j])
        k_all = kv[0, :slots, j].reshape(slots * 4 * rows, HD)
        v_all = kv[1, :slots, j].reshape(slots * 4 * rows, HD)
        for i in range(2):
            scores = lax.dot_general(
                qbuf[j, i], k_all, (((1,), (1,)), ((), ())), preferred_element_type=jnp.float32
            )
            shift = jnp.concatenate([bias[i, t:t + 1, :] for t in range(slots * 4)], axis=1)
            scores = scores * scale + shift
            peak = jnp.max(scores, axis=1, keepdims=True)
            unrounded = jnp.exp(scores - peak)
            total = jnp.sum(unrounded, axis=1, keepdims=True)
            summed = jnp.dot(unrounded.astype(jnp.bfloat16), v_all, preferred_element_type=jnp.float32)
            mine[j, i * rows:(i + 1) * rows, :] = (summed / total).astype(jnp.bfloat16)

    def attend(j):
        for i in range(2):
            arrived(qbuf.at[j, i], r_q.at[j, i])
            if j == 0:
                arrived(bias.at[i], r_b.at[i])
        pl.when(inner)(lambda: attend_slots(j, 3))
        pl.when(outer)(lambda: attend_slots(j, 2))
        for k in (2, 1, 3, 0):
            put(mine.at[j], att.at[z_odd, p, j], r_att.at[z_odd, p], (z + k) % 4, c, z_half)

    spread_own(0)
    spread_own(1)
    spread_beside(0)
    spread_own(2)
    spread_beside(1)
    for ct in (xn, yn):
        arrived(wide.at[ct], r_w.at[ct])
    passed = jnp.where(inner, xn, yn)
    push(wide.at[passed], wide.at[passed], r_w.at[passed], z, jnp.where(inner, yn, xn), p)
    spread_diagonal(0)
    attend(0)
    spread_beside(2)
    spread_diagonal(1)
    attend(1)
    spread_diagonal(2)
    attend(2)

    for zf in range(2):
        for half in range(2):
            arrived(att.at[zf, half], r_att.at[zf, half])
    arrived(wide.at[c], r_w.at[c])
    arrived(wide.at[dn], r_w.at[dn])

    def project(half):
        sums = [
            lax.dot_general(
                jnp.concatenate([att[zf, half, j] for j in range(heads)], axis=1),
                wide[:, :, zf * span:(zf + 1) * span].reshape(quarter, span),
                (((1,), (1,)), ((), ())), preferred_element_type=jnp.float32,
            )
            for zf in range(2)
        ]
        return (sums[0] + sums[1]).astype(jnp.bfloat16)

    part_out[...] = project(1 - p)
    push(part_out, part_in, r_part, z, c, 1 - p)
    own = project(p).astype(jnp.float32)
    arrived(part_in, r_part)
    staged[...] = (own + part_in[...].astype(jnp.float32)).astype(jnp.bfloat16)

    place = pl.ds(pl.multiple_of(z_odd * quarter, quarter), quarter)
    for i in range(2):
        put(staged.at[i * rows:(i + 1) * rows, :], o_ref.at[:, place], r_out.at[z_odd], 2 * p + i, c, z_half)
    for zf in range(2):
        arrived(o_ref.at[:, zf * quarter:(zf + 1) * quarter], r_out.at[zf])

    for when, copy in sent:
        if when is None:
            copy.wait_send()
        else:
            pl.when(when)(copy.wait_send)


def column_body(queries, keys, values, window, out_weight):
    rows, width = queries.shape
    depth, cols = out_weight.shape
    span = width // 2
    heads = span // HD
    bf16, f32 = jnp.bfloat16, jnp.float32
    dma = pltpu.SemaphoreType.DMA
    vmem = pl.BlockSpec(memory_space=pltpu.VMEM)
    hbm = pl.BlockSpec(memory_space=pltpu.HBM)
    copies = heads * (6 + 8 + 4) + 2 + 3 + 1 + 2
    return pl.pallas_call(
        column_kernel,
        out_shape=jax.ShapeDtypeStruct((rows, 8 * cols), bf16),
        in_specs=[hbm] * 5,
        out_specs=vmem,
        scratch_shapes=[
            pltpu.VMEM((1, window.shape[1]), jnp.int32),
            pltpu.VMEM((heads, 2, rows, HD), bf16),
            pltpu.VMEM((16, 128), f32),
            pltpu.VMEM((2, 16, 128), f32),
            pltpu.VMEM((2, 3, heads, 4, rows, HD), bf16),
            pltpu.VMEM((4, cols, depth), bf16),
            pltpu.VMEM((heads, 2 * rows, HD), bf16),
            pltpu.VMEM((2, 2, heads, 2 * rows, HD), bf16),
            pltpu.VMEM((2 * rows, 4 * cols), bf16),
            pltpu.VMEM((2 * rows, 4 * cols), bf16),
            pltpu.VMEM((2 * rows, 4 * cols), bf16),
            dma((copies,)), dma,
            dma((heads, 4)), dma((2, heads)), dma((3, heads)), dma((heads, 2)), dma((2,)), dma((4,)), dma((2, 2)), dma, dma((2,)),
        ],
        compiler_params=pltpu.CompilerParams(
            collective_id=0, has_side_effects=True, vmem_limit_bytes=64 * 1024 * 1024 - 65536
        ),
        cost_estimate=pl.CostEstimate(flops=1300000000, bytes_accessed=3000000, transcendentals=1200000),
    )(queries, keys, values, window, out_weight.T)


def solution(mesh):
    in_specs = (
        P("tok", "head"),
        P("tok", "head"),
        P("tok", "head"),
        P("tok", None),
        P("head", "tok"),
    )
    out_specs = P("tok", "head")
    small_grid = mesh.shape["tok"] == 16 and mesh.shape["head"] == 2
    body = column_body if small_grid else general_body
    return jax.shard_map(body, mesh=mesh, in_specs=in_specs, out_specs=out_specs, check_vma=False)
```

```python
import jax
import jax.numpy as jnp
from jax import lax
from jax.experimental import pallas as pl
from jax.experimental.pallas import tpu as pltpu
from jax.sharding import PartitionSpec as P

HD = 128
MESH = pl.DeviceIdType.MESH


def passed_along(value, axis, by):
    count = lax.axis_size(axis)
    pairs = [(i, i + by) for i in range(count) if 0 <= i + by < count]
    return lax.ppermute(value, axis, pairs)


def attend_tile(running, query_heads, kv_piece, is_listed):
    peak_now, total_now, summed_now = running
    tok_rows, head_count, head_size = query_heads.shape
    key_heads = kv_piece[0].reshape(tok_rows, head_count, head_size)
    value_heads = kv_piece[1].reshape(tok_rows, head_count, head_size)
    scores = jnp.einsum("qhd,khd->hqk", query_heads, key_heads, preferred_element_type=jnp.float32)
    scores = jnp.where(is_listed, scores * HD ** (-0.5), -1e30)
    new_peak = jnp.maximum(peak_now, jnp.max(scores, axis=-1))
    rescale = jnp.exp(peak_now - new_peak)
    unrounded = jnp.exp(scores - new_peak[..., None])
    total_next = total_now * rescale + jnp.sum(unrounded, axis=-1)
    weights = unrounded.astype(jnp.bfloat16)
    summed_next = summed_now * rescale[..., None] + jnp.einsum(
        "hqk,khd->hqd", weights, value_heads, preferred_element_type=jnp.float32
    )
    return (new_peak, total_next, summed_next)


def general_body(queries, keys, values, window, out_weight):
    tok_rows, feat_width = queries.shape
    head_count = feat_width // HD
    tile_count = lax.axis_size("tok")
    grid_w = min(8, tile_count // 4)
    grid_h = min(4, tile_count // (2 * grid_w))
    frame_size = grid_w * grid_h
    frame_count = tile_count // frame_size
    my_tile = lax.axis_index("tok")
    my_frame = my_tile // frame_size
    my_row = my_tile // grid_w % grid_h
    my_col = my_tile % grid_w
    query_heads = queries.reshape(tok_rows, head_count, HD)
    listed_tiles = window[0]
    initial = (
        jnp.full((head_count, tok_rows), -1e30, jnp.float32),
        jnp.zeros((head_count, tok_rows), jnp.float32),
        jnp.zeros((head_count, tok_rows, HD), jnp.float32),
    )
    own_pair = jnp.stack([keys, values])
    slot_blocks = []
    for step_f in (-1, 0, 1):
        for step_h in (-1, 0, 1):
            for step_w in (-1, 0, 1):
                distance = step_f * frame_size + step_h * grid_w + step_w
                if distance == 0:
                    slot_blocks.append(own_pair)
                else:
                    slot_blocks.append(passed_along(own_pair, "tok", -distance))
    near_box = jnp.stack(slot_blocks)
    slot_range = jnp.arange(27, dtype=jnp.int32)
    slot_f = slot_range // 9 - 1
    slot_h = slot_range // 3 % 3 - 1
    slot_w = slot_range % 3 - 1
    slot_distance = slot_f * frame_size + slot_h * grid_w + slot_w
    inside = (
        (my_frame + slot_f >= 0)
        & (my_frame + slot_f < frame_count)
        & (my_row + slot_h >= 0)
        & (my_row + slot_h < grid_h)
        & (my_col + slot_w >= 0)
        & (my_col + slot_w < grid_w)
    )

    def visit_band(running, slot_index):
        key_tile = my_tile + slot_distance[slot_index]
        is_listed = inside[slot_index] & jnp.any(listed_tiles == key_tile)
        kv_piece = lax.dynamic_index_in_dim(near_box, slot_index, 0, keepdims=False)
        return (attend_tile(running, query_heads, kv_piece, is_listed), None)

    running, _ = lax.scan(visit_band, initial, slot_range)
    attended = (running[2] / running[1][..., None]).transpose(1, 0, 2).reshape(tok_rows, feat_width)
    attended = attended.astype(jnp.bfloat16)
    projection = jnp.dot(
        attended,
        lax.all_gather(out_weight, "tok", axis=1, tiled=True),
        preferred_element_type=jnp.float32,
    )
    return lax.psum_scatter(
        projection.astype(jnp.bfloat16), "head", scatter_dimension=1, tiled=True
    )


def column_kernel(
    q_ref, k_ref, v_ref, win_ref, w_ref, o_ref,
    listing, qbuf, bias_own, bias, kv, wide, mine, att, part_out, part_in, staged, landed,
    send, s_win, r_x, r_plane, r_y, r_q, r_b, r_w, r_rev, r_att, r_part, r_out,
):
    tile = lax.axis_index("tok")
    p = lax.axis_index("head")
    z = tile // 4
    c = tile % 4
    z_half = z // 2
    z_odd = z % 2
    xn = c + 1 - 2 * (c % 2)
    yn = (c + 2) % 4
    zn = z + 1 - 2 * z_odd
    c_odd = c % 2
    member = z_odd * 2 + c_odd
    dn = 3 - c
    inner = (c == 1) | (c == 2)
    outer = jnp.logical_not(inner)
    rows = q_ref.shape[0]
    span = q_ref.shape[1] // 2
    heads = span // HD
    cols = w_ref.shape[0]
    scale = HD ** (-0.5)

    sent = []

    def remote(src, dst, rsem, zt, ct, ht):
        return pltpu.make_async_remote_copy(
            src_ref=src, dst_ref=dst, send_sem=send.at[len(sent)], recv_sem=rsem,
            device_id=(zt * 4 + ct, ht), device_id_type=MESH,
        )

    def push(src, dst, rsem, zt, ct, ht, when=None):
        copy = remote(src, dst, rsem, zt, ct, ht)
        if when is None:
            copy.start()
        else:
            pl.when(when)(copy.start)
        sent.append((when, copy))

    def put(src, dst, rsem, zt, ct, ht):
        here = (zt == z) & (ht == p)

        @pl.when(here)
        def _():
            pltpu.make_async_copy(src, dst, rsem).start()

        push(src, dst, rsem, zt, ct, ht, jnp.logical_not(here))

    def arrived(dst, rsem):
        pltpu.make_async_copy(dst, dst, rsem).wait()

    def lanes_of(j, base=0):
        return slice(base + j * HD, base + (j + 1) * HD)

    window_copy = pltpu.make_async_copy(win_ref, listing, s_win)
    window_copy.start()
    barrier = pltpu.get_barrier_semaphore()
    for k in range(1, 4):
        for h in range(2):
            pl.semaphore_signal(barrier, inc=1, device_id=((z + k) % 4 * 4 + c, h), device_id_type=MESH)
    for zt, ct in ((z, xn), (z, yn), (zn, xn)):
        pl.semaphore_signal(barrier, inc=1, device_id=(zt * 4 + ct, p), device_id_type=MESH)
    pl.semaphore_signal(barrier, inc=1, device_id=(tile, 1 - p), device_id_type=MESH)

    window_copy.wait()
    row = lax.broadcasted_iota(jnp.int32, (16, win_ref.shape[1]), 0)
    slot = row // 4
    column = jnp.where(slot == 0, c, jnp.where(slot == 1, xn, dn))
    key_tile = row % 4 * 4 + column
    listed = jnp.where(listing[...] == key_tile, 0.0, -1e30)
    bias_own[...] = jnp.broadcast_to(jnp.max(listed, axis=1, keepdims=True), bias_own.shape)

    pl.semaphore_wait(barrier, 10)

    for j in range(heads):
        for i in range(2):
            zd = 2 * p + i
            here = lanes_of(j, i * span)
            put(k_ref.at[:, here], kv.at[0, 0, j, z], r_x.at[j, z], zd, c, 0)
            put(v_ref.at[:, here], kv.at[1, 0, j, z], r_x.at[j, z], zd, c, 1)
            put(q_ref.at[:, here], qbuf.at[j, z_odd], r_q.at[j, z_odd], zd, c, z_half)
            if j == 0:
                put(bias_own, bias.at[z_odd], r_b.at[z_odd], zd, c, z_half)

    def share(s, j, when=None):
        push(kv.at[p, s, j], kv.at[p, s, j], r_y.at[s, j], z, c, 1 - p, when)

    def spread_own(j):
        for k in range(4):
            zz = (z + k) % 4
            piece = kv.at[p, 0, j, zz]
            arrived(piece, r_x.at[j, zz])
            push(piece, kv.at[p, 1, j, zz], r_plane.at[0, j], z, xn, p)
        share(0, j)

    def spread_beside(j):
        piece = kv.at[p, 1, j]
        arrived(piece, r_plane.at[0, j])
        push(piece, kv.at[p, 2, j], r_plane.at[1, j], z, yn, p, outer)
        share(1, j)

    def spread_diagonal(j):
        pl.when(inner)(lambda: arrived(kv.at[p, 2, j], r_plane.at[1, j]))
        share(2, j, inner)

    def attend_slots(j, slots):
        for s in range(slots):
            arrived(kv.at[1 - p, s, j], r_y.at[s, j])
        k_all = kv[0, :slots, j].reshape(slots * 4 * rows, HD)
        v_all = kv[1, :slots, j].reshape(slots * 4 * rows, HD)
        for i in range(2):
            scores = lax.dot_general(
                qbuf[j, i], k_all, (((1,), (1,)), ((), ())), preferred_element_type=jnp.float32
            )
            shift = jnp.concatenate([bias[i, t:t + 1, :] for t in range(slots * 4)], axis=1)
            scores = scores * scale + shift
            peak = jnp.max(scores, axis=1, keepdims=True)
            unrounded = jnp.exp(scores - peak)
            total = jnp.sum(unrounded, axis=1, keepdims=True)
            summed = jnp.dot(unrounded.astype(jnp.bfloat16), v_all, preferred_element_type=jnp.float32)
            mine[j, i] = (summed / total).astype(jnp.bfloat16)

    def attend(j):
        for i in range(2):
            arrived(qbuf.at[j, i], r_q.at[j, i])
            if j == 0:
                arrived(bias.at[i], r_b.at[i])
        pl.when(inner)(lambda: attend_slots(j, 3))
        pl.when(outer)(lambda: attend_slots(j, 2))
        for i in range(2):
            put(mine.at[j, i], att.at[i * 2 + c_odd, j, z_odd], r_rev.at[j, z_odd], 2 * p + i, c, z_half)

    def gather(j):
        for zf in range(2):
            arrived(att.at[member, j, zf], r_rev.at[j, zf])
        push(att.at[member, j], att.at[member, j], r_att.at[0, j], zn, c, p)
        push(att.at[member, j], att.at[member, j], r_att.at[1, j], z, xn, p)

    beside_z = (1 - z_odd) * 2 + c_odd
    beside_x = z_odd * 2 + 1 - c_odd
    across = 3 - member

    def relay(j):
        piece = att.at[beside_z, j]
        arrived(piece, r_att.at[0, j])
        push(piece, piece, r_att.at[2, j], z, xn, p)

    b = c // 2
    own_weight = wide.at[z_half, b]
    far_weight = wide.at[1 - z_half, b]

    push(w_ref, own_weight, r_w.at[z_half, b], z, yn, p)
    pltpu.make_async_copy(w_ref, own_weight, r_w.at[z_half, b]).start()
    spread_own(0)
    spread_own(1)
    spread_beside(0)
    spread_own(2)
    push(w_ref, own_weight, r_w.at[z_half, b], (z + 2) % 4, c, p)
    spread_beside(1)
    spread_diagonal(0)
    attend(0)
    spread_beside(2)
    spread_diagonal(1)
    attend(1)
    spread_diagonal(2)
    gather(0)
    attend(2)
    gather(1)
    relay(0)
    arrived(far_weight, r_w.at[1 - z_half, b])
    push(far_weight, far_weight, r_w.at[1 - z_half, b], z, yn, p)
    gather(2)
    relay(1)
    relay(2)

    arrived(own_weight, r_w.at[z_half, b])
    for a in range(2):
        arrived(wide.at[a, 1 - b], r_w.at[a, 1 - b])
    for j in range(heads):
        arrived(att.at[beside_x, j], r_att.at[1, j])
        arrived(att.at[across, j], r_att.at[2, j])

    def project(a):
        attended = jnp.concatenate(
            [att[:, j, zf].reshape(4 * rows, HD) for zf in range(2) for j in range(heads)], axis=1
        )
        columns = wide[a].reshape(2 * cols, 2 * span)
        return lax.dot_general(
            attended, columns, (((1,), (1,)), ((), ())), preferred_element_type=jnp.float32
        ).astype(jnp.bfloat16)

    part_out[...] = project(1 - p)
    push(part_out, part_in, r_part, z, c, 1 - p)
    own = project(p).astype(jnp.float32)
    arrived(part_in, r_part)
    staged[...] = (own + part_in[...].astype(jnp.float32)).astype(jnp.bfloat16).reshape(staged.shape)

    push(staged.at[across], landed.at[member], r_out.at[member], zn, xn, p)
    push(staged.at[beside_x], landed.at[member], r_out.at[member], z, xn, p)
    push(staged.at[beside_z], landed.at[member], r_out.at[member], zn, c, p)
    landed[member] = staged[member]
    for m in range(4):
        pl.when(member != m)(lambda: arrived(landed.at[m], r_out.at[m]))
        for b_out in range(2):
            first = (m // 2 * 4 + b_out * 2 + m % 2) * cols
            o_ref[:, first:first + cols] = landed[m, :, b_out * cols:(b_out + 1) * cols]

    for when, copy in sent:
        if when is None:
            copy.wait_send()
        else:
            pl.when(when)(copy.wait_send)


def column_body(queries, keys, values, window, out_weight):
    rows, width = queries.shape
    depth, cols = out_weight.shape
    span = width // 2
    heads = span // HD
    bf16, f32 = jnp.bfloat16, jnp.float32
    dma = pltpu.SemaphoreType.DMA
    vmem = pl.BlockSpec(memory_space=pltpu.VMEM)
    hbm = pl.BlockSpec(memory_space=pltpu.HBM)
    copies = heads * (6 + 8 + 2 + 3) + 2 + 3 + 1 + 3
    return pl.pallas_call(
        column_kernel,
        out_shape=jax.ShapeDtypeStruct((rows, 8 * cols), bf16),
        in_specs=[hbm] * 5,
        out_specs=vmem,
        scratch_shapes=[
            pltpu.VMEM((1, window.shape[1]), jnp.int32),
            pltpu.VMEM((heads, 2, rows, HD), bf16),
            pltpu.VMEM((16, 128), f32),
            pltpu.VMEM((2, 16, 128), f32),
            pltpu.VMEM((2, 3, heads, 4, rows, HD), bf16),
            pltpu.VMEM((2, 2, cols, depth), bf16),
            pltpu.VMEM((heads, 2, rows, HD), bf16),
            pltpu.VMEM((4, heads, 2, rows, HD), bf16),
            pltpu.VMEM((4 * rows, 2 * cols), bf16),
            pltpu.VMEM((4 * rows, 2 * cols), bf16),
            pltpu.VMEM((4, rows, 2 * cols), bf16),
            pltpu.VMEM((4, rows, 2 * cols), bf16),
            dma((copies,)), dma,
            dma((heads, 4)), dma((2, heads)), dma((3, heads)), dma((heads, 2)), dma((2,)), dma((2, 2)),
            dma((heads, 2)), dma((3, heads)), dma, dma((4,)),
        ],
        compiler_params=pltpu.CompilerParams(
            collective_id=0, has_side_effects=True, vmem_limit_bytes=64 * 1024 * 1024 - 65536
        ),
        cost_estimate=pl.CostEstimate(flops=1300000000, bytes_accessed=3000000, transcendentals=1200000),
    )(queries, keys, values, window, out_weight.T)


def solution(mesh):
    in_specs = (
        P("tok", "head"),
        P("tok", "head"),
        P("tok", "head"),
        P("tok", None),
        P("head", "tok"),
    )
    out_specs = P("tok", "head")
    small_grid = mesh.shape["tok"] == 16 and mesh.shape["head"] == 2
    body = column_body if small_grid else general_body
    return jax.shard_map(body, mesh=mesh, in_specs=in_specs, out_specs=out_specs, check_vma=False)
```

```python
import jax
import jax.numpy as jnp
from jax import lax
from jax.experimental import pallas as pl
from jax.experimental.pallas import tpu as pltpu
from jax.sharding import PartitionSpec as P

HD = 128
LOG2E = 1.4426950408889634
MESH = pl.DeviceIdType.MESH


def passed_along(value, axis, by):
    count = lax.axis_size(axis)
    pairs = [(i, i + by) for i in range(count) if 0 <= i + by < count]
    return lax.ppermute(value, axis, pairs)


def attend_tile(running, query_heads, kv_piece, is_listed):
    peak_now, total_now, summed_now = running
    tok_rows, head_count, head_size = query_heads.shape
    key_heads = kv_piece[0].reshape(tok_rows, head_count, head_size)
    value_heads = kv_piece[1].reshape(tok_rows, head_count, head_size)
    scores = jnp.einsum("qhd,khd->hqk", query_heads, key_heads, preferred_element_type=jnp.float32)
    scores = jnp.where(is_listed, scores * HD ** (-0.5), -1e30)
    new_peak = jnp.maximum(peak_now, jnp.max(scores, axis=-1))
    rescale = jnp.exp(peak_now - new_peak)
    unrounded = jnp.exp(scores - new_peak[..., None])
    total_next = total_now * rescale + jnp.sum(unrounded, axis=-1)
    weights = unrounded.astype(jnp.bfloat16)
    summed_next = summed_now * rescale[..., None] + jnp.einsum(
        "hqk,khd->hqd", weights, value_heads, preferred_element_type=jnp.float32
    )
    return (new_peak, total_next, summed_next)


def general_body(queries, keys, values, window, out_weight):
    tok_rows, feat_width = queries.shape
    head_count = feat_width // HD
    tile_count = lax.axis_size("tok")
    grid_w = min(8, tile_count // 4)
    grid_h = min(4, tile_count // (2 * grid_w))
    frame_size = grid_w * grid_h
    frame_count = tile_count // frame_size
    my_tile = lax.axis_index("tok")
    my_frame = my_tile // frame_size
    my_row = my_tile // grid_w % grid_h
    my_col = my_tile % grid_w
    query_heads = queries.reshape(tok_rows, head_count, HD)
    listed_tiles = window[0]
    initial = (
        jnp.full((head_count, tok_rows), -1e30, jnp.float32),
        jnp.zeros((head_count, tok_rows), jnp.float32),
        jnp.zeros((head_count, tok_rows, HD), jnp.float32),
    )
    own_pair = jnp.stack([keys, values])
    slot_blocks = []
    for step_f in (-1, 0, 1):
        for step_h in (-1, 0, 1):
            for step_w in (-1, 0, 1):
                distance = step_f * frame_size + step_h * grid_w + step_w
                if distance == 0:
                    slot_blocks.append(own_pair)
                else:
                    slot_blocks.append(passed_along(own_pair, "tok", -distance))
    near_box = jnp.stack(slot_blocks)
    slot_range = jnp.arange(27, dtype=jnp.int32)
    slot_f = slot_range // 9 - 1
    slot_h = slot_range // 3 % 3 - 1
    slot_w = slot_range % 3 - 1
    slot_distance = slot_f * frame_size + slot_h * grid_w + slot_w
    inside = (
        (my_frame + slot_f >= 0)
        & (my_frame + slot_f < frame_count)
        & (my_row + slot_h >= 0)
        & (my_row + slot_h < grid_h)
        & (my_col + slot_w >= 0)
        & (my_col + slot_w < grid_w)
    )

    def visit_band(running, slot_index):
        key_tile = my_tile + slot_distance[slot_index]
        is_listed = inside[slot_index] & jnp.any(listed_tiles == key_tile)
        kv_piece = lax.dynamic_index_in_dim(near_box, slot_index, 0, keepdims=False)
        return (attend_tile(running, query_heads, kv_piece, is_listed), None)

    running, _ = lax.scan(visit_band, initial, slot_range)
    attended = (running[2] / running[1][..., None]).transpose(1, 0, 2).reshape(tok_rows, feat_width)
    attended = attended.astype(jnp.bfloat16)
    projection = jnp.dot(
        attended,
        lax.all_gather(out_weight, "tok", axis=1, tiled=True),
        preferred_element_type=jnp.float32,
    )
    return lax.psum_scatter(
        projection.astype(jnp.bfloat16), "head", scatter_dimension=1, tiled=True
    )


def column_kernel(
    q_ref, k_ref, v_ref, win_ref, w_ref, o_ref,
    listing, qbuf, bias_own, bias, kv, wide, mine, att, near_sum, part_out, part_in, staged,
    send, s_win, r_x, r_plane, r_y, r_q, r_b, r_w, r_att, r_part, r_out,
):
    tile = lax.axis_index("tok")
    p = lax.axis_index("head")
    z = tile // 4
    c = tile % 4
    z_half = z // 2
    z_odd = z % 2
    xn = c + 1 - 2 * (c % 2)
    yn = (c + 2) % 4
    dn = 3 - c
    inner = (c == 1) | (c == 2)
    outer = jnp.logical_not(inner)
    rows = q_ref.shape[0]
    span = q_ref.shape[1] // 2
    heads = span // HD
    quarter = 4 * w_ref.shape[0]
    scale = HD ** (-0.5) * LOG2E

    sent = []

    def remote(src, dst, rsem, zt, ct, ht):
        return pltpu.make_async_remote_copy(
            src_ref=src, dst_ref=dst, send_sem=send.at[len(sent)], recv_sem=rsem,
            device_id=(zt * 4 + ct, ht), device_id_type=MESH,
        )

    def push(src, dst, rsem, zt, ct, ht, when=None):
        copy = remote(src, dst, rsem, zt, ct, ht)
        if when is None:
            copy.start()
        else:
            pl.when(when)(copy.start)
        sent.append((when, copy))

    def put(src, dst, rsem, zt, ct, ht):
        here = (zt == z) & (ht == p)

        @pl.when(here)
        def _():
            pltpu.make_async_copy(src, dst, rsem).start()

        push(src, dst, rsem, zt, ct, ht, jnp.logical_not(here))

    def arrived(dst, rsem):
        pltpu.make_async_copy(dst, dst, rsem).wait()

    def lanes_of(j, base=0):
        return slice(base + j * HD, base + (j + 1) * HD)

    window_copy = pltpu.make_async_copy(win_ref, listing, s_win)
    window_copy.start()
    barrier = pltpu.get_barrier_semaphore()
    for k in range(1, 4):
        for h in range(2):
            pl.semaphore_signal(barrier, inc=1, device_id=((z + k) % 4 * 4 + c, h), device_id_type=MESH)
    for ct in (xn, yn):
        pl.semaphore_signal(barrier, inc=1, device_id=(z * 4 + ct, p), device_id_type=MESH)
    pl.semaphore_signal(barrier, inc=1, device_id=(tile, 1 - p), device_id_type=MESH)

    window_copy.wait()
    row = lax.broadcasted_iota(jnp.int32, (16, win_ref.shape[1]), 0)
    slot = row // 4
    column = jnp.where(slot == 0, c, jnp.where(slot == 1, xn, dn))
    key_tile = row % 4 * 4 + column
    listed = jnp.where(listing[...] == key_tile, 0.0, -1e30)
    bias_own[...] = jnp.broadcast_to(jnp.max(listed, axis=1, keepdims=True), bias_own.shape)

    pl.semaphore_wait(barrier, 9)

    def send_line(j):
        for i in range(2):
            zd = 2 * p + i
            here = lanes_of(j, i * span)
            put(k_ref.at[:, here], kv.at[0, 0, j, z], r_x.at[j, z], zd, c, 0)
            put(v_ref.at[:, here], kv.at[1, 0, j, z], r_x.at[j, z], zd, c, 1)
            put(q_ref.at[:, here], qbuf.at[j, z_odd], r_q.at[j, z_odd], zd, c, z_half)
            if j == 0:
                put(bias_own, bias.at[z_odd], r_b.at[z_odd], zd, c, z_half)

    def share(s, j, when=None):
        push(kv.at[p, s, j], kv.at[p, s, j], r_y.at[s, j], z, c, 1 - p, when)

    def spread_own(j):
        for k in range(4):
            zz = (z + k) % 4
            piece = kv.at[p, 0, j, zz]
            arrived(piece, r_x.at[j, zz])
            push(piece, kv.at[p, 1, j, zz], r_plane.at[0, j], z, xn, p)
        share(0, j)

    def spread_beside(j):
        piece = kv.at[p, 1, j]
        arrived(piece, r_plane.at[0, j])
        push(piece, kv.at[p, 2, j], r_plane.at[1, j], z, yn, p, outer)
        share(1, j)

    def spread_diagonal(j):
        pl.when(inner)(lambda: arrived(kv.at[p, 2, j], r_plane.at[1, j]))
        share(2, j, inner)

    def attend_slots(j, slots):
        for s in range(slots):
            arrived(kv.at[1 - p, s, j], r_y.at[s, j])
        k_all = kv[0, :slots, j].reshape(slots * 4 * rows, HD)
        v_all = kv[1, :slots, j].reshape(slots * 4 * rows, HD)
        both = lax.dot_general(
            qbuf[j].reshape(2 * rows, HD), k_all, (((1,), (1,)), ((), ())), preferred_element_type=jnp.float32
        )
        for i in range(2):
            shift = jnp.concatenate([bias[i, t:t + 1, :] for t in range(slots * 4)], axis=1)
            scores = both[i * rows:(i + 1) * rows, :] * scale + shift
            peak = jnp.max(scores, axis=1, keepdims=True)
            unrounded = jnp.exp2(scores - peak)
            total = jnp.sum(unrounded, axis=1, keepdims=True)
            summed = jnp.dot(unrounded.astype(jnp.bfloat16), v_all, preferred_element_type=jnp.float32)
            mine[j, i * rows:(i + 1) * rows, :] = (summed / total).astype(jnp.bfloat16)

    def attend(j):
        for i in range(2):
            arrived(qbuf.at[j, i], r_q.at[j, i])
            if j == 0:
                arrived(bias.at[i], r_b.at[i])
        pl.when(inner)(lambda: attend_slots(j, 3))
        pl.when(outer)(lambda: attend_slots(j, 2))
        for k in (2, 1, 3, 0):
            put(mine.at[j], att.at[z_odd, p, j], r_att.at[z_odd, p], (z + k) % 4, c, z_half)

    send_line(0)
    send_line(1)
    spread_own(0)
    send_line(2)
    spread_own(1)
    for ct in (xn, yn):
        push(w_ref, wide.at[c], r_w.at[c], z, ct, p)
    pltpu.make_async_copy(w_ref, wide.at[c], r_w.at[c]).start()
    spread_beside(0)
    spread_own(2)
    spread_beside(1)
    spread_diagonal(0)
    attend(0)
    spread_beside(2)
    spread_diagonal(1)
    attend(1)
    for ct in (xn, yn):
        arrived(wide.at[ct], r_w.at[ct])
    passed = jnp.where(inner, xn, yn)
    push(wide.at[passed], wide.at[passed], r_w.at[passed], z, jnp.where(inner, yn, xn), p)
    spread_diagonal(2)
    attend(2)
    arrived(wide.at[c], r_w.at[c])
    arrived(wide.at[dn], r_w.at[dn])

    near = jnp.where(z > 2 * p, 1, 0)

    def features(zf, half):
        arrived(att.at[zf, half], r_att.at[zf, half])
        return jnp.concatenate([att[zf, half, j] for j in range(heads)], axis=1)

    def times_weight(attended, zf):
        columns = wide[:, :, pl.ds(pl.multiple_of(zf * span, span), span)].reshape(quarter, span)
        return lax.dot_general(attended, columns, (((1,), (1,)), ((), ())), preferred_element_type=jnp.float32)

    for half in range(2):
        near_sum[half] = times_weight(features(near, half), near)

    def project(half):
        return (near_sum[half] + times_weight(features(1 - near, half), 1 - near)).astype(jnp.bfloat16)

    part_out[...] = project(1 - p)
    push(part_out, part_in, r_part, z, c, 1 - p)
    own = project(p).astype(jnp.float32)
    arrived(part_in, r_part)
    staged[...] = (own + part_in[...].astype(jnp.float32)).astype(jnp.bfloat16)

    place = pl.ds(pl.multiple_of(z_odd * quarter, quarter), quarter)
    for i in range(2):
        put(staged.at[i * rows:(i + 1) * rows, :], o_ref.at[:, place], r_out.at[z_odd], 2 * p + i, c, z_half)
    for zf in range(2):
        arrived(o_ref.at[:, zf * quarter:(zf + 1) * quarter], r_out.at[zf])

    for when, copy in sent:
        if when is None:
            copy.wait_send()
        else:
            pl.when(when)(copy.wait_send)


def column_body(queries, keys, values, window, out_weight):
    rows, width = queries.shape
    depth, cols = out_weight.shape
    span = width // 2
    heads = span // HD
    bf16, f32 = jnp.bfloat16, jnp.float32
    dma = pltpu.SemaphoreType.DMA
    vmem = pl.BlockSpec(memory_space=pltpu.VMEM)
    hbm = pl.BlockSpec(memory_space=pltpu.HBM)
    copies = heads * (6 + 8 + 4) + 2 + 3 + 1 + 2
    return pl.pallas_call(
        column_kernel,
        out_shape=jax.ShapeDtypeStruct((rows, 8 * cols), bf16),
        in_specs=[hbm] * 5,
        out_specs=vmem,
        scratch_shapes=[
            pltpu.VMEM((1, window.shape[1]), jnp.int32),
            pltpu.VMEM((heads, 2, rows, HD), bf16),
            pltpu.VMEM((16, 128), f32),
            pltpu.VMEM((2, 16, 128), f32),
            pltpu.VMEM((2, 3, heads, 4, rows, HD), bf16),
            pltpu.VMEM((4, cols, depth), bf16),
            pltpu.VMEM((heads, 2 * rows, HD), bf16),
            pltpu.VMEM((2, 2, heads, 2 * rows, HD), bf16),
            pltpu.VMEM((2, 2 * rows, 4 * cols), f32),
            pltpu.VMEM((2 * rows, 4 * cols), bf16),
            pltpu.VMEM((2 * rows, 4 * cols), bf16),
            pltpu.VMEM((2 * rows, 4 * cols), bf16),
            dma((copies,)), dma,
            dma((heads, 4)), dma((2, heads)), dma((3, heads)), dma((heads, 2)), dma((2,)), dma((4,)), dma((2, 2)), dma, dma((2,)),
        ],
        compiler_params=pltpu.CompilerParams(
            collective_id=0, has_side_effects=True, vmem_limit_bytes=64 * 1024 * 1024 - 65536
        ),
        cost_estimate=pl.CostEstimate(flops=1300000000, bytes_accessed=3000000, transcendentals=1200000),
    )(queries, keys, values, window, out_weight.T)


def solution(mesh):
    in_specs = (
        P("tok", "head"),
        P("tok", "head"),
        P("tok", "head"),
        P("tok", None),
        P("head", "tok"),
    )
    out_specs = P("tok", "head")
    small_grid = mesh.shape["tok"] == 16 and mesh.shape["head"] == 2
    body = column_body if small_grid else general_body
    return jax.shard_map(body, mesh=mesh, in_specs=in_specs, out_specs=out_specs, check_vma=False)
```

```python
import jax
import jax.numpy as jnp
from jax import lax
from jax.experimental import pallas as pl
from jax.experimental.pallas import tpu as pltpu
from jax.sharding import PartitionSpec as P

HD = 128
LOG2E = 1.4426950408889634
MESH = pl.DeviceIdType.MESH


def passed_along(value, axis, by):
    count = lax.axis_size(axis)
    pairs = [(i, i + by) for i in range(count) if 0 <= i + by < count]
    return lax.ppermute(value, axis, pairs)


def attend_tile(running, query_heads, kv_piece, is_listed):
    peak_now, total_now, summed_now = running
    tok_rows, head_count, head_size = query_heads.shape
    key_heads = kv_piece[0].reshape(tok_rows, head_count, head_size)
    value_heads = kv_piece[1].reshape(tok_rows, head_count, head_size)
    scores = jnp.einsum("qhd,khd->hqk", query_heads, key_heads, preferred_element_type=jnp.float32)
    scores = jnp.where(is_listed, scores * HD ** (-0.5), -1e30)
    new_peak = jnp.maximum(peak_now, jnp.max(scores, axis=-1))
    rescale = jnp.exp(peak_now - new_peak)
    unrounded = jnp.exp(scores - new_peak[..., None])
    total_next = total_now * rescale + jnp.sum(unrounded, axis=-1)
    weights = unrounded.astype(jnp.bfloat16)
    summed_next = summed_now * rescale[..., None] + jnp.einsum(
        "hqk,khd->hqd", weights, value_heads, preferred_element_type=jnp.float32
    )
    return (new_peak, total_next, summed_next)


def general_body(queries, keys, values, window, out_weight):
    tok_rows, feat_width = queries.shape
    head_count = feat_width // HD
    tile_count = lax.axis_size("tok")
    grid_w = min(8, tile_count // 4)
    grid_h = min(4, tile_count // (2 * grid_w))
    frame_size = grid_w * grid_h
    frame_count = tile_count // frame_size
    my_tile = lax.axis_index("tok")
    my_frame = my_tile // frame_size
    my_row = my_tile // grid_w % grid_h
    my_col = my_tile % grid_w
    query_heads = queries.reshape(tok_rows, head_count, HD)
    listed_tiles = window[0]
    initial = (
        jnp.full((head_count, tok_rows), -1e30, jnp.float32),
        jnp.zeros((head_count, tok_rows), jnp.float32),
        jnp.zeros((head_count, tok_rows, HD), jnp.float32),
    )
    own_pair = jnp.stack([keys, values])
    slot_blocks = []
    for step_f in (-1, 0, 1):
        for step_h in (-1, 0, 1):
            for step_w in (-1, 0, 1):
                distance = step_f * frame_size + step_h * grid_w + step_w
                if distance == 0:
                    slot_blocks.append(own_pair)
                else:
                    slot_blocks.append(passed_along(own_pair, "tok", -distance))
    near_box = jnp.stack(slot_blocks)
    slot_range = jnp.arange(27, dtype=jnp.int32)
    slot_f = slot_range // 9 - 1
    slot_h = slot_range // 3 % 3 - 1
    slot_w = slot_range % 3 - 1
    slot_distance = slot_f * frame_size + slot_h * grid_w + slot_w
    inside = (
        (my_frame + slot_f >= 0)
        & (my_frame + slot_f < frame_count)
        & (my_row + slot_h >= 0)
        & (my_row + slot_h < grid_h)
        & (my_col + slot_w >= 0)
        & (my_col + slot_w < grid_w)
    )

    def visit_band(running, slot_index):
        key_tile = my_tile + slot_distance[slot_index]
        is_listed = inside[slot_index] & jnp.any(listed_tiles == key_tile)
        kv_piece = lax.dynamic_index_in_dim(near_box, slot_index, 0, keepdims=False)
        return (attend_tile(running, query_heads, kv_piece, is_listed), None)

    running, _ = lax.scan(visit_band, initial, slot_range)
    attended = (running[2] / running[1][..., None]).transpose(1, 0, 2).reshape(tok_rows, feat_width)
    attended = attended.astype(jnp.bfloat16)
    projection = jnp.dot(
        attended,
        lax.all_gather(out_weight, "tok", axis=1, tiled=True),
        preferred_element_type=jnp.float32,
    )
    return lax.psum_scatter(
        projection.astype(jnp.bfloat16), "head", scatter_dimension=1, tiled=True
    )


def column_kernel(
    q_ref, k_ref, v_ref, win_ref, w_ref, o_ref,
    listing, qbuf, bias_own, bias, kv, wide, mine, att, near_sum, part_out, part_in, staged,
    send, s_win, r_x, r_plane, r_y, r_q, r_b, r_w, r_att, r_part, r_out,
):
    tile = lax.axis_index("tok")
    p = lax.axis_index("head")
    z = tile // 4
    c = tile % 4
    z_half = z // 2
    z_odd = z % 2
    xn = c + 1 - 2 * (c % 2)
    yn = (c + 2) % 4
    dn = 3 - c
    inner = (c == 1) | (c == 2)
    outer = jnp.logical_not(inner)
    rows = q_ref.shape[0]
    span = q_ref.shape[1] // 2
    heads = span // HD
    quarter = 4 * w_ref.shape[0]
    scale = HD ** (-0.5) * LOG2E

    sent = []

    def remote(src, dst, rsem, zt, ct, ht):
        return pltpu.make_async_remote_copy(
            src_ref=src, dst_ref=dst, send_sem=send.at[len(sent)], recv_sem=rsem,
            device_id=(zt * 4 + ct, ht), device_id_type=MESH,
        )

    def push(src, dst, rsem, zt, ct, ht, when=None):
        copy = remote(src, dst, rsem, zt, ct, ht)
        if when is None:
            copy.start()
        else:
            pl.when(when)(copy.start)
        sent.append((when, copy))

    def put(src, dst, rsem, zt, ct, ht):
        here = (zt == z) & (ht == p)

        @pl.when(here)
        def _():
            pltpu.make_async_copy(src, dst, rsem).start()

        push(src, dst, rsem, zt, ct, ht, jnp.logical_not(here))

    def arrived(dst, rsem):
        pltpu.make_async_copy(dst, dst, rsem).wait()

    def lanes_of(j, base=0):
        return slice(base + j * HD, base + (j + 1) * HD)

    window_copy = pltpu.make_async_copy(win_ref, listing, s_win)
    window_copy.start()
    barrier = pltpu.get_barrier_semaphore()
    for k in range(1, 4):
        for h in range(2):
            pl.semaphore_signal(barrier, inc=1, device_id=((z + k) % 4 * 4 + c, h), device_id_type=MESH)
    for ct in (xn, yn):
        pl.semaphore_signal(barrier, inc=1, device_id=(z * 4 + ct, p), device_id_type=MESH)
    pl.semaphore_signal(barrier, inc=1, device_id=(tile, 1 - p), device_id_type=MESH)

    window_copy.wait()
    row = lax.broadcasted_iota(jnp.int32, (16, win_ref.shape[1]), 0)
    slot = row // 4
    column = jnp.where(slot == 0, c, jnp.where(slot == 1, xn, dn))
    key_tile = row % 4 * 4 + column
    listed = jnp.where(listing[...] == key_tile, 0.0, -1e30)
    bias_own[...] = jnp.broadcast_to(jnp.max(listed, axis=1, keepdims=True), bias_own.shape)

    pl.semaphore_wait(barrier, 9)

    def send_line(j):
        for i in range(2):
            zd = 2 * p + i
            here = lanes_of(j, i * span)
            put(k_ref.at[:, here], kv.at[0, 0, j, z], r_x.at[j, z], zd, c, 0)
            put(v_ref.at[:, here], kv.at[1, 0, j, z], r_x.at[j, z], zd, c, 1)
            put(q_ref.at[:, here], qbuf.at[j, z_odd], r_q.at[j, z_odd], zd, c, z_half)
            if j == 0:
                put(bias_own, bias.at[z_odd], r_b.at[z_odd], zd, c, z_half)

    def share(s, j, when=None):
        push(kv.at[p, s, j], kv.at[p, s, j], r_y.at[s, j], z, c, 1 - p, when)

    def spread_own(j):
        for k in range(4):
            zz = (z + k) % 4
            piece = kv.at[p, 0, j, zz]
            arrived(piece, r_x.at[j, zz])
            push(piece, kv.at[p, 1, j, zz], r_plane.at[0, j], z, xn, p)
        share(0, j)

    def spread_beside(j):
        piece = kv.at[p, 1, j]
        arrived(piece, r_plane.at[0, j])
        push(piece, kv.at[p, 2, j], r_plane.at[1, j], z, yn, p, outer)
        share(1, j)

    def spread_diagonal(j):
        pl.when(inner)(lambda: arrived(kv.at[p, 2, j], r_plane.at[1, j]))
        share(2, j, inner)

    def attend_slots(j, slots):
        for s in range(slots):
            arrived(kv.at[1 - p, s, j], r_y.at[s, j])
        k_all = kv[0, :slots, j].reshape(slots * 4 * rows, HD)
        v_all = kv[1, :slots, j].reshape(slots * 4 * rows, HD)
        for i in range(2):
            scores = lax.dot_general(
                qbuf[j, i], k_all, (((1,), (1,)), ((), ())), preferred_element_type=jnp.float32
            )
            shift = jnp.concatenate([bias[i, t:t + 1, :] for t in range(slots * 4)], axis=1)
            scores = scores * scale + shift
            peak = jnp.max(scores, axis=1, keepdims=True)
            unrounded = jnp.exp2(scores - peak)
            total = jnp.sum(unrounded, axis=1, keepdims=True)
            summed = jnp.dot(unrounded.astype(jnp.bfloat16), v_all, preferred_element_type=jnp.float32)
            mine[j, i * rows:(i + 1) * rows, :] = (summed / total).astype(jnp.bfloat16)

    def attend(j):
        for i in range(2):
            arrived(qbuf.at[j, i], r_q.at[j, i])
            if j == 0:
                arrived(bias.at[i], r_b.at[i])
        pl.when(inner)(lambda: attend_slots(j, 3))
        pl.when(outer)(lambda: attend_slots(j, 2))
        for k in (2, 1, 3, 0):
            put(mine.at[j], att.at[z_odd, p, j], r_att.at[z_odd, p], (z + k) % 4, c, z_half)

    for ct in (xn, yn):
        push(w_ref, wide.at[c], r_w.at[c], z, ct, p)
    pltpu.make_async_copy(w_ref, wide.at[c], r_w.at[c]).start()
    send_line(0)
    send_line(1)
    send_line(2)
    spread_own(0)
    spread_own(1)
    spread_beside(0)
    spread_own(2)
    spread_beside(1)
    for ct in (xn, yn):
        arrived(wide.at[ct], r_w.at[ct])
    passed = jnp.where(inner, xn, yn)
    push(wide.at[passed], wide.at[passed], r_w.at[passed], z, jnp.where(inner, yn, xn), p)
    spread_diagonal(0)
    attend(0)
    spread_beside(2)
    spread_diagonal(1)
    attend(1)
    spread_diagonal(2)
    attend(2)
    arrived(wide.at[c], r_w.at[c])
    arrived(wide.at[dn], r_w.at[dn])

    near = jnp.where(z > 2 * p, 1, 0)

    def features(zf, half):
        arrived(att.at[zf, half], r_att.at[zf, half])
        return jnp.concatenate([att[zf, half, j] for j in range(heads)], axis=1)

    def times_weight(attended, zf):
        columns = wide[:, :, pl.ds(pl.multiple_of(zf * span, span), span)].reshape(quarter, span)
        return lax.dot_general(attended, columns, (((1,), (1,)), ((), ())), preferred_element_type=jnp.float32)

    for half in range(2):
        near_sum[half] = times_weight(features(near, half), near)

    def project(half):
        return (near_sum[half] + times_weight(features(1 - near, half), 1 - near)).astype(jnp.bfloat16)

    part_out[...] = project(1 - p)
    push(part_out, part_in, r_part, z, c, 1 - p)
    own = project(p).astype(jnp.float32)
    arrived(part_in, r_part)
    staged[...] = (own + part_in[...].astype(jnp.float32)).astype(jnp.bfloat16)

    place = pl.ds(pl.multiple_of(z_odd * quarter, quarter), quarter)
    for i in range(2):
        put(staged.at[i * rows:(i + 1) * rows, :], o_ref.at[:, place], r_out.at[z_odd], 2 * p + i, c, z_half)
    for zf in range(2):
        arrived(o_ref.at[:, zf * quarter:(zf + 1) * quarter], r_out.at[zf])

    for when, copy in sent:
        if when is None:
            copy.wait_send()
        else:
            pl.when(when)(copy.wait_send)


def column_body(queries, keys, values, window, out_weight):
    rows, width = queries.shape
    depth, cols = out_weight.shape
    span = width // 2
    heads = span // HD
    bf16, f32 = jnp.bfloat16, jnp.float32
    dma = pltpu.SemaphoreType.DMA
    vmem = pl.BlockSpec(memory_space=pltpu.VMEM)
    hbm = pl.BlockSpec(memory_space=pltpu.HBM)
    copies = heads * (6 + 8 + 4) + 2 + 3 + 1 + 2
    return pl.pallas_call(
        column_kernel,
        out_shape=jax.ShapeDtypeStruct((rows, 8 * cols), bf16),
        in_specs=[hbm] * 5,
        out_specs=vmem,
        scratch_shapes=[
            pltpu.VMEM((1, window.shape[1]), jnp.int32),
            pltpu.VMEM((heads, 2, rows, HD), bf16),
            pltpu.VMEM((16, 128), f32),
            pltpu.VMEM((2, 16, 128), f32),
            pltpu.VMEM((2, 3, heads, 4, rows, HD), bf16),
            pltpu.VMEM((4, cols, depth), bf16),
            pltpu.VMEM((heads, 2 * rows, HD), bf16),
            pltpu.VMEM((2, 2, heads, 2 * rows, HD), bf16),
            pltpu.VMEM((2, 2 * rows, 4 * cols), f32),
            pltpu.VMEM((2 * rows, 4 * cols), bf16),
            pltpu.VMEM((2 * rows, 4 * cols), bf16),
            pltpu.VMEM((2 * rows, 4 * cols), bf16),
            dma((copies,)), dma,
            dma((heads, 4)), dma((2, heads)), dma((3, heads)), dma((heads, 2)), dma((2,)), dma((4,)), dma((2, 2)), dma, dma((2,)),
        ],
        compiler_params=pltpu.CompilerParams(
            collective_id=0, has_side_effects=True, vmem_limit_bytes=64 * 1024 * 1024 - 65536
        ),
        cost_estimate=pl.CostEstimate(flops=1300000000, bytes_accessed=3000000, transcendentals=1200000),
    )(queries, keys, values, window, out_weight.T)


def solution(mesh):
    in_specs = (
        P("tok", "head"),
        P("tok", "head"),
        P("tok", "head"),
        P("tok", None),
        P("head", "tok"),
    )
    out_specs = P("tok", "head")
    small_grid = mesh.shape["tok"] == 16 and mesh.shape["head"] == 2
    body = column_body if small_grid else general_body
    return jax.shard_map(body, mesh=mesh, in_specs=in_specs, out_specs=out_specs, check_vma=False)
```

```python
import jax
import jax.numpy as jnp
from jax import lax
from jax.experimental import pallas as pl
from jax.experimental.pallas import tpu as pltpu
from jax.sharding import PartitionSpec as P

HD = 128
LOG2E = 1.4426950408889634
MESH = pl.DeviceIdType.MESH


def passed_along(value, axis, by):
    count = lax.axis_size(axis)
    pairs = [(i, i + by) for i in range(count) if 0 <= i + by < count]
    return lax.ppermute(value, axis, pairs)


def attend_tile(running, query_heads, kv_piece, is_listed):
    peak_now, total_now, summed_now = running
    tok_rows, head_count, head_size = query_heads.shape
    key_heads = kv_piece[0].reshape(tok_rows, head_count, head_size)
    value_heads = kv_piece[1].reshape(tok_rows, head_count, head_size)
    scores = jnp.einsum("qhd,khd->hqk", query_heads, key_heads, preferred_element_type=jnp.float32)
    scores = jnp.where(is_listed, scores * HD ** (-0.5), -1e30)
    new_peak = jnp.maximum(peak_now, jnp.max(scores, axis=-1))
    rescale = jnp.exp(peak_now - new_peak)
    unrounded = jnp.exp(scores - new_peak[..., None])
    total_next = total_now * rescale + jnp.sum(unrounded, axis=-1)
    weights = unrounded.astype(jnp.bfloat16)
    summed_next = summed_now * rescale[..., None] + jnp.einsum(
        "hqk,khd->hqd", weights, value_heads, preferred_element_type=jnp.float32
    )
    return (new_peak, total_next, summed_next)


def general_body(queries, keys, values, window, out_weight):
    tok_rows, feat_width = queries.shape
    head_count = feat_width // HD
    tile_count = lax.axis_size("tok")
    grid_w = min(8, tile_count // 4)
    grid_h = min(4, tile_count // (2 * grid_w))
    frame_size = grid_w * grid_h
    frame_count = tile_count // frame_size
    my_tile = lax.axis_index("tok")
    my_frame = my_tile // frame_size
    my_row = my_tile // grid_w % grid_h
    my_col = my_tile % grid_w
    query_heads = queries.reshape(tok_rows, head_count, HD)
    listed_tiles = window[0]
    initial = (
        jnp.full((head_count, tok_rows), -1e30, jnp.float32),
        jnp.zeros((head_count, tok_rows), jnp.float32),
        jnp.zeros((head_count, tok_rows, HD), jnp.float32),
    )
    own_pair = jnp.stack([keys, values])
    slot_blocks = []
    for step_f in (-1, 0, 1):
        for step_h in (-1, 0, 1):
            for step_w in (-1, 0, 1):
                distance = step_f * frame_size + step_h * grid_w + step_w
                if distance == 0:
                    slot_blocks.append(own_pair)
                else:
                    slot_blocks.append(passed_along(own_pair, "tok", -distance))
    near_box = jnp.stack(slot_blocks)
    slot_range = jnp.arange(27, dtype=jnp.int32)
    slot_f = slot_range // 9 - 1
    slot_h = slot_range // 3 % 3 - 1
    slot_w = slot_range % 3 - 1
    slot_distance = slot_f * frame_size + slot_h * grid_w + slot_w
    inside = (
        (my_frame + slot_f >= 0)
        & (my_frame + slot_f < frame_count)
        & (my_row + slot_h >= 0)
        & (my_row + slot_h < grid_h)
        & (my_col + slot_w >= 0)
        & (my_col + slot_w < grid_w)
    )

    def visit_band(running, slot_index):
        key_tile = my_tile + slot_distance[slot_index]
        is_listed = inside[slot_index] & jnp.any(listed_tiles == key_tile)
        kv_piece = lax.dynamic_index_in_dim(near_box, slot_index, 0, keepdims=False)
        return (attend_tile(running, query_heads, kv_piece, is_listed), None)

    running, _ = lax.scan(visit_band, initial, slot_range)
    attended = (running[2] / running[1][..., None]).transpose(1, 0, 2).reshape(tok_rows, feat_width)
    attended = attended.astype(jnp.bfloat16)
    projection = jnp.dot(
        attended,
        lax.all_gather(out_weight, "tok", axis=1, tiled=True),
        preferred_element_type=jnp.float32,
    )
    return lax.psum_scatter(
        projection.astype(jnp.bfloat16), "head", scatter_dimension=1, tiled=True
    )


def column_kernel(
    q_ref, k_ref, v_ref, win_ref, w_ref, o_ref,
    listing, qbuf, bias_own, bias, kv, wide, mine, att, near_sum, part_out, part_in, staged,
    send, s_win, r_x, r_plane, r_y, r_q, r_b, r_w, r_att, r_part, r_out,
):
    tile = lax.axis_index("tok")
    p = lax.axis_index("head")
    z = tile // 4
    c = tile % 4
    z_half = z // 2
    z_odd = z % 2
    xn = c + 1 - 2 * (c % 2)
    yn = (c + 2) % 4
    dn = 3 - c
    inner = (c == 1) | (c == 2)
    outer = jnp.logical_not(inner)
    rows = q_ref.shape[0]
    span = q_ref.shape[1] // 2
    heads = span // HD
    quarter = 4 * w_ref.shape[0]
    scale = HD ** (-0.5) * LOG2E

    sent = []

    def remote(src, dst, rsem, zt, ct, ht):
        return pltpu.make_async_remote_copy(
            src_ref=src, dst_ref=dst, send_sem=send.at[len(sent)], recv_sem=rsem,
            device_id=(zt * 4 + ct, ht), device_id_type=MESH,
        )

    def push(src, dst, rsem, zt, ct, ht, when=None):
        copy = remote(src, dst, rsem, zt, ct, ht)
        if when is None:
            copy.start()
        else:
            pl.when(when)(copy.start)
        sent.append((when, copy))

    def put(src, dst, rsem, zt, ct, ht):
        here = (zt == z) & (ht == p)

        @pl.when(here)
        def _():
            pltpu.make_async_copy(src, dst, rsem).start()

        push(src, dst, rsem, zt, ct, ht, jnp.logical_not(here))

    def arrived(dst, rsem):
        pltpu.make_async_copy(dst, dst, rsem).wait()

    def lanes_of(j, base=0):
        return slice(base + j * HD, base + (j + 1) * HD)

    window_copy = pltpu.make_async_copy(win_ref, listing, s_win)
    window_copy.start()
    barrier = pltpu.get_barrier_semaphore()
    for k in range(1, 4):
        for h in range(2):
            pl.semaphore_signal(barrier, inc=1, device_id=((z + k) % 4 * 4 + c, h), device_id_type=MESH)
    for ct in (xn, yn):
        pl.semaphore_signal(barrier, inc=1, device_id=(z * 4 + ct, p), device_id_type=MESH)
    pl.semaphore_signal(barrier, inc=1, device_id=(tile, 1 - p), device_id_type=MESH)

    window_copy.wait()
    row = lax.broadcasted_iota(jnp.int32, (16, win_ref.shape[1]), 0)
    slot = row // 4
    column = jnp.where(slot == 0, c, jnp.where(slot == 1, xn, dn))
    key_tile = row % 4 * 4 + column
    listed = jnp.where(listing[...] == key_tile, 0.0, -1e30)
    bias_own[...] = jnp.broadcast_to(jnp.max(listed, axis=1, keepdims=True), bias_own.shape)

    pl.semaphore_wait(barrier, 9)

    def send_line(j):
        for i in range(2):
            zd = 2 * p + i
            here = lanes_of(j, i * span)
            put(k_ref.at[:, here], kv.at[0, 0, j, z], r_x.at[j, z], zd, c, 0)
            put(v_ref.at[:, here], kv.at[1, 0, j, z], r_x.at[j, z], zd, c, 1)
            put(q_ref.at[:, here], qbuf.at[j, z_odd], r_q.at[j, z_odd], zd, c, z_half)
            if j == 0:
                put(bias_own, bias.at[z_odd], r_b.at[z_odd], zd, c, z_half)

    def share(s, j, when=None):
        push(kv.at[p, s, j], kv.at[p, s, j], r_y.at[s, j], z, c, 1 - p, when)

    def spread_own(j):
        for k in range(4):
            zz = (z + k) % 4
            piece = kv.at[p, 0, j, zz]
            arrived(piece, r_x.at[j, zz])
            push(piece, kv.at[p, 1, j, zz], r_plane.at[0, j], z, xn, p)
        share(0, j)

    def spread_beside(j):
        piece = kv.at[p, 1, j]
        arrived(piece, r_plane.at[0, j])
        push(piece, kv.at[p, 2, j], r_plane.at[1, j], z, yn, p, outer)
        share(1, j)

    def spread_diagonal(j):
        pl.when(inner)(lambda: arrived(kv.at[p, 2, j], r_plane.at[1, j]))
        share(2, j, inner)

    def attend_slots(j, slots):
        for s in range(slots):
            arrived(kv.at[1 - p, s, j], r_y.at[s, j])
        k_all = kv[0, :slots, j].reshape(slots * 4 * rows, HD)
        v_all = kv[1, :slots, j].reshape(slots * 4 * rows, HD)
        for i in range(2):
            scores = lax.dot_general(
                qbuf[j, i], k_all, (((1,), (1,)), ((), ())), preferred_element_type=jnp.float32
            )
            shift = jnp.concatenate([bias[i, t:t + 1, :] for t in range(slots * 4)], axis=1)
            scores = scores * scale + shift
            peak = jnp.max(scores, axis=1, keepdims=True)
            unrounded = jnp.exp2(scores - peak)
            total = jnp.sum(unrounded, axis=1, keepdims=True)
            summed = jnp.dot(unrounded.astype(jnp.bfloat16), v_all, preferred_element_type=jnp.float32)
            mine[j, i * rows:(i + 1) * rows, :] = (summed / total).astype(jnp.bfloat16)

    def attend(j):
        for i in range(2):
            arrived(qbuf.at[j, i], r_q.at[j, i])
            if j == 0:
                arrived(bias.at[i], r_b.at[i])
        pl.when(inner)(lambda: attend_slots(j, 3))
        pl.when(outer)(lambda: attend_slots(j, 2))
        beyond = jnp.where(z_half == 0, 2, 1)
        for zt in (beyond, z + 1 - 2 * z_odd, z):
            put(mine.at[j], att.at[z_odd, p, j], r_att.at[z_odd, p, j], zt, c, z_half)

    hands_on = ((z == 1) & (p == 1)) | ((z == 2) & (p == 0))
    end = jnp.where(z == 1, 0, 3)

    def hand_on(j):
        for zf in (p, 1 - p):
            for half in range(2):
                piece = att.at[1 - zf, half, j]
                pl.when(hands_on)(lambda: arrived(piece, r_att.at[1 - zf, half, j]))
                push(piece, piece, r_att.at[1 - zf, half, j], end, c, p, hands_on)

    for ct in (xn, yn):
        push(w_ref, wide.at[c], r_w.at[c], z, ct, p)
    pltpu.make_async_copy(w_ref, wide.at[c], r_w.at[c]).start()
    send_line(0)
    send_line(1)
    send_line(2)
    spread_own(0)
    spread_own(1)
    spread_beside(0)
    spread_own(2)
    spread_beside(1)
    for ct in (xn, yn):
        arrived(wide.at[ct], r_w.at[ct])
    passed = jnp.where(inner, xn, yn)
    push(wide.at[passed], wide.at[passed], r_w.at[passed], z, jnp.where(inner, yn, xn), p)
    spread_diagonal(0)
    attend(0)
    spread_beside(2)
    spread_diagonal(1)
    attend(1)
    spread_diagonal(2)
    hand_on(0)
    attend(2)
    hand_on(1)
    hand_on(2)
    arrived(wide.at[c], r_w.at[c])
    arrived(wide.at[dn], r_w.at[dn])

    near = jnp.where(z > 2 * p, 1, 0)

    def features(zf, half):

        @pl.when(jnp.logical_not(hands_on))
        def _():
            for j in range(heads):
                arrived(att.at[zf, half, j], r_att.at[zf, half, j])

        return jnp.concatenate([att[zf, half, j] for j in range(heads)], axis=1)

    def times_weight(attended, zf):
        columns = wide[:, :, pl.ds(pl.multiple_of(zf * span, span), span)].reshape(quarter, span)
        return lax.dot_general(attended, columns, (((1,), (1,)), ((), ())), preferred_element_type=jnp.float32)

    for half in range(2):
        near_sum[half] = times_weight(features(near, half), near)

    def project(half):
        return (near_sum[half] + times_weight(features(1 - near, half), 1 - near)).astype(jnp.bfloat16)

    part_out[...] = project(1 - p)
    push(part_out, part_in, r_part, z, c, 1 - p)
    own = project(p).astype(jnp.float32)
    arrived(part_in, r_part)
    staged[...] = (own + part_in[...].astype(jnp.float32)).astype(jnp.bfloat16)

    place = pl.ds(pl.multiple_of(z_odd * quarter, quarter), quarter)
    for i in range(2):
        put(staged.at[i * rows:(i + 1) * rows, :], o_ref.at[:, place], r_out.at[z_odd], 2 * p + i, c, z_half)
    for zf in range(2):
        arrived(o_ref.at[:, zf * quarter:(zf + 1) * quarter], r_out.at[zf])

    for when, copy in sent:
        if when is None:
            copy.wait_send()
        else:
            pl.when(when)(copy.wait_send)


def column_body(queries, keys, values, window, out_weight):
    rows, width = queries.shape
    depth, cols = out_weight.shape
    span = width // 2
    heads = span // HD
    bf16, f32 = jnp.bfloat16, jnp.float32
    dma = pltpu.SemaphoreType.DMA
    vmem = pl.BlockSpec(memory_space=pltpu.VMEM)
    hbm = pl.BlockSpec(memory_space=pltpu.HBM)
    copies = heads * (6 + 8 + 3 + 4) + 2 + 3 + 1 + 2
    return pl.pallas_call(
        column_kernel,
        out_shape=jax.ShapeDtypeStruct((rows, 8 * cols), bf16),
        in_specs=[hbm] * 5,
        out_specs=vmem,
        scratch_shapes=[
            pltpu.VMEM((1, window.shape[1]), jnp.int32),
            pltpu.VMEM((heads, 2, rows, HD), bf16),
            pltpu.VMEM((16, 128), f32),
            pltpu.VMEM((2, 16, 128), f32),
            pltpu.VMEM((2, 3, heads, 4, rows, HD), bf16),
            pltpu.VMEM((4, cols, depth), bf16),
            pltpu.VMEM((heads, 2 * rows, HD), bf16),
            pltpu.VMEM((2, 2, heads, 2 * rows, HD), bf16),
            pltpu.VMEM((2, 2 * rows, 4 * cols), f32),
            pltpu.VMEM((2 * rows, 4 * cols), bf16),
            pltpu.VMEM((2 * rows, 4 * cols), bf16),
            pltpu.VMEM((2 * rows, 4 * cols), bf16),
            dma((copies,)), dma,
            dma((heads, 4)), dma((2, heads)), dma((3, heads)), dma((heads, 2)), dma((2,)), dma((4,)), dma((2, 2, heads)), dma, dma((2,)),
        ],
        compiler_params=pltpu.CompilerParams(
            collective_id=0, has_side_effects=True, vmem_limit_bytes=64 * 1024 * 1024 - 65536
        ),
        cost_estimate=pl.CostEstimate(flops=1300000000, bytes_accessed=3000000, transcendentals=1200000),
    )(queries, keys, values, window, out_weight.T)


def solution(mesh):
    in_specs = (
        P("tok", "head"),
        P("tok", "head"),
        P("tok", "head"),
        P("tok", None),
        P("head", "tok"),
    )
    out_specs = P("tok", "head")
    small_grid = mesh.shape["tok"] == 16 and mesh.shape["head"] == 2
    body = column_body if small_grid else general_body
    return jax.shard_map(body, mesh=mesh, in_specs=in_specs, out_specs=out_specs, check_vma=False)
```

```python
import jax
import jax.numpy as jnp
from jax import lax
from jax.experimental import pallas as pl
from jax.experimental.pallas import tpu as pltpu
from jax.sharding import PartitionSpec as P

HD = 128
LOG2E = 1.4426950408889634
MESH = pl.DeviceIdType.MESH


def passed_along(value, axis, by):
    count = lax.axis_size(axis)
    pairs = [(i, i + by) for i in range(count) if 0 <= i + by < count]
    return lax.ppermute(value, axis, pairs)


def attend_tile(running, query_heads, kv_piece, is_listed):
    peak_now, total_now, summed_now = running
    tok_rows, head_count, head_size = query_heads.shape
    key_heads = kv_piece[0].reshape(tok_rows, head_count, head_size)
    value_heads = kv_piece[1].reshape(tok_rows, head_count, head_size)
    scores = jnp.einsum("qhd,khd->hqk", query_heads, key_heads, preferred_element_type=jnp.float32)
    scores = jnp.where(is_listed, scores * HD ** (-0.5), -1e30)
    new_peak = jnp.maximum(peak_now, jnp.max(scores, axis=-1))
    rescale = jnp.exp(peak_now - new_peak)
    unrounded = jnp.exp(scores - new_peak[..., None])
    total_next = total_now * rescale + jnp.sum(unrounded, axis=-1)
    weights = unrounded.astype(jnp.bfloat16)
    summed_next = summed_now * rescale[..., None] + jnp.einsum(
        "hqk,khd->hqd", weights, value_heads, preferred_element_type=jnp.float32
    )
    return (new_peak, total_next, summed_next)


def general_body(queries, keys, values, window, out_weight):
    tok_rows, feat_width = queries.shape
    head_count = feat_width // HD
    tile_count = lax.axis_size("tok")
    grid_w = min(8, tile_count // 4)
    grid_h = min(4, tile_count // (2 * grid_w))
    frame_size = grid_w * grid_h
    frame_count = tile_count // frame_size
    my_tile = lax.axis_index("tok")
    my_frame = my_tile // frame_size
    my_row = my_tile // grid_w % grid_h
    my_col = my_tile % grid_w
    query_heads = queries.reshape(tok_rows, head_count, HD)
    listed_tiles = window[0]
    initial = (
        jnp.full((head_count, tok_rows), -1e30, jnp.float32),
        jnp.zeros((head_count, tok_rows), jnp.float32),
        jnp.zeros((head_count, tok_rows, HD), jnp.float32),
    )
    own_pair = jnp.stack([keys, values])
    slot_blocks = []
    for step_f in (-1, 0, 1):
        for step_h in (-1, 0, 1):
            for step_w in (-1, 0, 1):
                distance = step_f * frame_size + step_h * grid_w + step_w
                if distance == 0:
                    slot_blocks.append(own_pair)
                else:
                    slot_blocks.append(passed_along(own_pair, "tok", -distance))
    near_box = jnp.stack(slot_blocks)
    slot_range = jnp.arange(27, dtype=jnp.int32)
    slot_f = slot_range // 9 - 1
    slot_h = slot_range // 3 % 3 - 1
    slot_w = slot_range % 3 - 1
    slot_distance = slot_f * frame_size + slot_h * grid_w + slot_w
    inside = (
        (my_frame + slot_f >= 0)
        & (my_frame + slot_f < frame_count)
        & (my_row + slot_h >= 0)
        & (my_row + slot_h < grid_h)
        & (my_col + slot_w >= 0)
        & (my_col + slot_w < grid_w)
    )

    def visit_band(running, slot_index):
        key_tile = my_tile + slot_distance[slot_index]
        is_listed = inside[slot_index] & jnp.any(listed_tiles == key_tile)
        kv_piece = lax.dynamic_index_in_dim(near_box, slot_index, 0, keepdims=False)
        return (attend_tile(running, query_heads, kv_piece, is_listed), None)

    running, _ = lax.scan(visit_band, initial, slot_range)
    attended = (running[2] / running[1][..., None]).transpose(1, 0, 2).reshape(tok_rows, feat_width)
    attended = attended.astype(jnp.bfloat16)
    projection = jnp.dot(
        attended,
        lax.all_gather(out_weight, "tok", axis=1, tiled=True),
        preferred_element_type=jnp.float32,
    )
    return lax.psum_scatter(
        projection.astype(jnp.bfloat16), "head", scatter_dimension=1, tiled=True
    )


def column_kernel(
    q_ref, k_ref, v_ref, win_ref, w_ref, o_ref,
    listing, qbuf, bias_own, bias, kv, wide, mine, att, near_sum, part_out, part_in, staged,
    send, s_win, r_x, r_plane, r_y, r_q, r_b, r_w, r_att, r_part, r_out,
):
    tile = lax.axis_index("tok")
    p = lax.axis_index("head")
    z = tile // 4
    c = tile % 4
    z_half = z // 2
    z_odd = z % 2
    xn = c + 1 - 2 * (c % 2)
    yn = (c + 2) % 4
    dn = 3 - c
    inner = (c == 1) | (c == 2)
    outer = jnp.logical_not(inner)
    rows = q_ref.shape[0]
    span = q_ref.shape[1] // 2
    heads = span // HD
    quarter = 4 * w_ref.shape[0]
    scale = HD ** (-0.5) * LOG2E

    sent = []

    def remote(src, dst, rsem, zt, ct, ht):
        return pltpu.make_async_remote_copy(
            src_ref=src, dst_ref=dst, send_sem=send.at[len(sent)], recv_sem=rsem,
            device_id=(zt * 4 + ct, ht), device_id_type=MESH,
        )

    def push(src, dst, rsem, zt, ct, ht, when=None):
        copy = remote(src, dst, rsem, zt, ct, ht)
        if when is None:
            copy.start()
        else:
            pl.when(when)(copy.start)
        sent.append((when, copy))

    def put(src, dst, rsem, zt, ct, ht):
        here = (zt == z) & (ht == p)

        @pl.when(here)
        def _():
            pltpu.make_async_copy(src, dst, rsem).start()

        push(src, dst, rsem, zt, ct, ht, jnp.logical_not(here))

    def arrived(dst, rsem):
        pltpu.make_async_copy(dst, dst, rsem).wait()

    def lanes_of(j, base=0):
        return slice(base + j * HD, base + (j + 1) * HD)

    window_copy = pltpu.make_async_copy(win_ref, listing, s_win)
    window_copy.start()
    barrier = pltpu.get_barrier_semaphore()
    for k in range(1, 4):
        for h in range(2):
            pl.semaphore_signal(barrier, inc=1, device_id=((z + k) % 4 * 4 + c, h), device_id_type=MESH)
    for ct in (xn, yn):
        pl.semaphore_signal(barrier, inc=1, device_id=(z * 4 + ct, p), device_id_type=MESH)
    pl.semaphore_signal(barrier, inc=1, device_id=(tile, 1 - p), device_id_type=MESH)

    window_copy.wait()
    row = lax.broadcasted_iota(jnp.int32, (16, win_ref.shape[1]), 0)
    slot = row // 4
    column = jnp.where(slot == 0, c, jnp.where(slot == 1, xn, dn))
    key_tile = row % 4 * 4 + column
    listed = jnp.where(listing[...] == key_tile, 0.0, -1e30)
    bias_own[...] = jnp.broadcast_to(jnp.max(listed, axis=1, keepdims=True), bias_own.shape)

    pl.semaphore_wait(barrier, 9)

    def send_line(j):
        for i in range(2):
            zd = 2 * p + i
            here = lanes_of(j, i * span)
            put(k_ref.at[:, here], kv.at[0, 0, j, z], r_x.at[j, z], zd, c, 0)
            put(v_ref.at[:, here], kv.at[1, 0, j, z], r_x.at[j, z], zd, c, 1)
            put(q_ref.at[:, here], qbuf.at[j, z_odd], r_q.at[j, z_odd], zd, c, z_half)
            if j == 0:
                put(bias_own, bias.at[z_odd], r_b.at[z_odd], zd, c, z_half)

    def share(s, j, when=None):
        push(kv.at[p, s, j], kv.at[p, s, j], r_y.at[s, j], z, c, 1 - p, when)

    def spread_own(j):
        for zz in (z, z + 1 - 2 * z_odd, 2 - z_half, 3 - 3 * z_half):
            piece = kv.at[p, 0, j, zz]
            arrived(piece, r_x.at[j, zz])
            push(piece, kv.at[p, 1, j, zz], r_plane.at[0, j], z, xn, p)
        share(0, j)

    def spread_beside(j):
        piece = kv.at[p, 1, j]
        arrived(piece, r_plane.at[0, j])
        push(piece, kv.at[p, 2, j], r_plane.at[1, j], z, yn, p, outer)
        share(1, j)

    def spread_diagonal(j):
        pl.when(inner)(lambda: arrived(kv.at[p, 2, j], r_plane.at[1, j]))
        share(2, j, inner)

    def attend_slots(j, slots):
        for s in range(slots):
            arrived(kv.at[1 - p, s, j], r_y.at[s, j])
        k_all = kv[0, :slots, j].reshape(slots * 4 * rows, HD)
        v_all = kv[1, :slots, j].reshape(slots * 4 * rows, HD)
        for i in range(2):
            scores = lax.dot_general(
                qbuf[j, i], k_all, (((1,), (1,)), ((), ())), preferred_element_type=jnp.float32
            )
            shift = jnp.concatenate([bias[i, t:t + 1, :] for t in range(slots * 4)], axis=1)
            scores = scores * scale + shift
            peak = jnp.max(scores, axis=1, keepdims=True)
            unrounded = jnp.exp2(scores - peak)
            total = jnp.sum(unrounded, axis=1, keepdims=True)
            summed = jnp.dot(unrounded.astype(jnp.bfloat16), v_all, preferred_element_type=jnp.float32)
            mine[j, i * rows:(i + 1) * rows, :] = (summed / total).astype(jnp.bfloat16)

    def attend(j):
        for i in range(2):
            arrived(qbuf.at[j, i], r_q.at[j, i])
            if j == 0:
                arrived(bias.at[i], r_b.at[i])
        pl.when(inner)(lambda: attend_slots(j, 3))
        pl.when(outer)(lambda: attend_slots(j, 2))
        beyond = jnp.where(z_half == 0, 2, 1)
        for zt in (beyond, z + 1 - 2 * z_odd, z):
            put(mine.at[j], att.at[z_odd, p, j], r_att.at[z_odd, p, j], zt, c, z_half)

    hands_on = ((z == 1) & (p == 1)) | ((z == 2) & (p == 0))
    end = jnp.where(z == 1, 0, 3)

    def hand_on(j):
        for zf in (p, 1 - p):
            for half in range(2):
                piece = att.at[1 - zf, half, j]
                pl.when(hands_on)(lambda: arrived(piece, r_att.at[1 - zf, half, j]))
                push(piece, piece, r_att.at[1 - zf, half, j], end, c, p, hands_on)

    for ct in (xn, yn):
        push(w_ref, wide.at[c], r_w.at[c], z, ct, p)
    pltpu.make_async_copy(w_ref, wide.at[c], r_w.at[c]).start()
    send_line(0)
    send_line(1)
    send_line(2)
    spread_own(0)
    spread_own(1)
    spread_beside(0)
    spread_own(2)
    spread_beside(1)
    spread_diagonal(0)
    attend(0)
    spread_beside(2)
    for ct in (xn, yn):
        arrived(wide.at[ct], r_w.at[ct])
    passed = jnp.where(inner, xn, yn)
    push(wide.at[passed], wide.at[passed], r_w.at[passed], z, jnp.where(inner, yn, xn), p)
    spread_diagonal(1)
    attend(1)
    spread_diagonal(2)
    hand_on(0)
    attend(2)
    hand_on(1)
    hand_on(2)
    arrived(wide.at[c], r_w.at[c])
    arrived(wide.at[dn], r_w.at[dn])

    near = jnp.where(z > 2 * p, 1, 0)

    def features(zf, half):

        @pl.when(jnp.logical_not(hands_on))
        def _():
            for j in range(heads):
                arrived(att.at[zf, half, j], r_att.at[zf, half, j])

        return jnp.concatenate([att[zf, half, j] for j in range(heads)], axis=1)

    def times_weight(attended, zf):
        columns = wide[:, :, pl.ds(pl.multiple_of(zf * span, span), span)].reshape(quarter, span)
        return lax.dot_general(attended, columns, (((1,), (1,)), ((), ())), preferred_element_type=jnp.float32)

    for half in range(2):
        near_sum[half] = times_weight(features(near, half), near)

    def project(half):
        return (near_sum[half] + times_weight(features(1 - near, half), 1 - near)).astype(jnp.bfloat16)

    part_out[...] = project(1 - p)
    push(part_out, part_in, r_part, z, c, 1 - p)
    own = project(p).astype(jnp.float32)
    arrived(part_in, r_part)

    place = pl.ds(pl.multiple_of(z_odd * quarter, quarter), quarter)
    for i in range(2):
        mid = slice(i * rows, (i + 1) * rows)
        staged[mid, :] = (own[mid, :] + part_in[mid, :].astype(jnp.float32)).astype(jnp.bfloat16)
        put(staged.at[mid, :], o_ref.at[:, place], r_out.at[z_odd], 2 * p + i, c, z_half)
    for zf in range(2):
        arrived(o_ref.at[:, zf * quarter:(zf + 1) * quarter], r_out.at[zf])

    for when, copy in sent:
        if when is None:
            copy.wait_send()
        else:
            pl.when(when)(copy.wait_send)


def column_body(queries, keys, values, window, out_weight):
    rows, width = queries.shape
    depth, cols = out_weight.shape
    span = width // 2
    heads = span // HD
    bf16, f32 = jnp.bfloat16, jnp.float32
    dma = pltpu.SemaphoreType.DMA
    hbm = pl.BlockSpec(memory_space=pltpu.HBM)
    copies = heads * (6 + 8 + 3 + 4) + 2 + 3 + 1 + 2
    return pl.pallas_call(
        column_kernel,
        out_shape=jax.ShapeDtypeStruct((rows, 8 * cols), bf16),
        in_specs=[hbm] * 5,
        out_specs=hbm,
        scratch_shapes=[
            pltpu.VMEM((1, window.shape[1]), jnp.int32),
            pltpu.VMEM((heads, 2, rows, HD), bf16),
            pltpu.VMEM((16, 128), f32),
            pltpu.VMEM((2, 16, 128), f32),
            pltpu.VMEM((2, 3, heads, 4, rows, HD), bf16),
            pltpu.VMEM((4, cols, depth), bf16),
            pltpu.VMEM((heads, 2 * rows, HD), bf16),
            pltpu.VMEM((2, 2, heads, 2 * rows, HD), bf16),
            pltpu.VMEM((2, 2 * rows, 4 * cols), f32),
            pltpu.VMEM((2 * rows, 4 * cols), bf16),
            pltpu.VMEM((2 * rows, 4 * cols), bf16),
            pltpu.VMEM((2 * rows, 4 * cols), bf16),
            dma((copies,)), dma,
            dma((heads, 4)), dma((2, heads)), dma((3, heads)), dma((heads, 2)), dma((2,)), dma((4,)), dma((2, 2, heads)), dma, dma((2,)),
        ],
        compiler_params=pltpu.CompilerParams(
            collective_id=0, has_side_effects=True, vmem_limit_bytes=64 * 1024 * 1024 - 65536
        ),
        cost_estimate=pl.CostEstimate(flops=1300000000, bytes_accessed=3000000, transcendentals=1200000),
    )(queries, keys, values, window, out_weight.T)


def solution(mesh):
    in_specs = (
        P("tok", "head"),
        P("tok", "head"),
        P("tok", "head"),
        P("tok", None),
        P("head", "tok"),
    )
    out_specs = P("tok", "head")
    small_grid = mesh.shape["tok"] == 16 and mesh.shape["head"] == 2
    body = column_body if small_grid else general_body
    return jax.shard_map(body, mesh=mesh, in_specs=in_specs, out_specs=out_specs, check_vma=False)
```

```python
import jax
import jax.numpy as jnp
from jax import lax
from jax.experimental import pallas as pl
from jax.experimental.pallas import tpu as pltpu
from jax.sharding import PartitionSpec as P

HD = 128
LOG2E = 1.4426950408889634
MESH = pl.DeviceIdType.MESH


def passed_along(value, axis, by):
    count = lax.axis_size(axis)
    pairs = [(i, i + by) for i in range(count) if 0 <= i + by < count]
    return lax.ppermute(value, axis, pairs)


def attend_tile(running, query_heads, kv_piece, is_listed):
    peak_now, total_now, summed_now = running
    tok_rows, head_count, head_size = query_heads.shape
    key_heads = kv_piece[0].reshape(tok_rows, head_count, head_size)
    value_heads = kv_piece[1].reshape(tok_rows, head_count, head_size)
    scores = jnp.einsum("qhd,khd->hqk", query_heads, key_heads, preferred_element_type=jnp.float32)
    scores = jnp.where(is_listed, scores * HD ** (-0.5), -1e30)
    new_peak = jnp.maximum(peak_now, jnp.max(scores, axis=-1))
    rescale = jnp.exp(peak_now - new_peak)
    unrounded = jnp.exp(scores - new_peak[..., None])
    total_next = total_now * rescale + jnp.sum(unrounded, axis=-1)
    weights = unrounded.astype(jnp.bfloat16)
    summed_next = summed_now * rescale[..., None] + jnp.einsum(
        "hqk,khd->hqd", weights, value_heads, preferred_element_type=jnp.float32
    )
    return (new_peak, total_next, summed_next)


def general_body(queries, keys, values, window, out_weight):
    tok_rows, feat_width = queries.shape
    head_count = feat_width // HD
    tile_count = lax.axis_size("tok")
    grid_w = min(8, tile_count // 4)
    grid_h = min(4, tile_count // (2 * grid_w))
    frame_size = grid_w * grid_h
    frame_count = tile_count // frame_size
    my_tile = lax.axis_index("tok")
    my_frame = my_tile // frame_size
    my_row = my_tile // grid_w % grid_h
    my_col = my_tile % grid_w
    query_heads = queries.reshape(tok_rows, head_count, HD)
    listed_tiles = window[0]
    initial = (
        jnp.full((head_count, tok_rows), -1e30, jnp.float32),
        jnp.zeros((head_count, tok_rows), jnp.float32),
        jnp.zeros((head_count, tok_rows, HD), jnp.float32),
    )
    own_pair = jnp.stack([keys, values])
    slot_blocks = []
    for step_f in (-1, 0, 1):
        for step_h in (-1, 0, 1):
            for step_w in (-1, 0, 1):
                distance = step_f * frame_size + step_h * grid_w + step_w
                if distance == 0:
                    slot_blocks.append(own_pair)
                else:
                    slot_blocks.append(passed_along(own_pair, "tok", -distance))
    near_box = jnp.stack(slot_blocks)
    slot_range = jnp.arange(27, dtype=jnp.int32)
    slot_f = slot_range // 9 - 1
    slot_h = slot_range // 3 % 3 - 1
    slot_w = slot_range % 3 - 1
    slot_distance = slot_f * frame_size + slot_h * grid_w + slot_w
    inside = (
        (my_frame + slot_f >= 0)
        & (my_frame + slot_f < frame_count)
        & (my_row + slot_h >= 0)
        & (my_row + slot_h < grid_h)
        & (my_col + slot_w >= 0)
        & (my_col + slot_w < grid_w)
    )

    def visit_band(running, slot_index):
        key_tile = my_tile + slot_distance[slot_index]
        is_listed = inside[slot_index] & jnp.any(listed_tiles == key_tile)
        kv_piece = lax.dynamic_index_in_dim(near_box, slot_index, 0, keepdims=False)
        return (attend_tile(running, query_heads, kv_piece, is_listed), None)

    running, _ = lax.scan(visit_band, initial, slot_range)
    attended = (running[2] / running[1][..., None]).transpose(1, 0, 2).reshape(tok_rows, feat_width)
    attended = attended.astype(jnp.bfloat16)
    projection = jnp.dot(
        attended,
        lax.all_gather(out_weight, "tok", axis=1, tiled=True),
        preferred_element_type=jnp.float32,
    )
    return lax.psum_scatter(
        projection.astype(jnp.bfloat16), "head", scatter_dimension=1, tiled=True
    )


def column_kernel(
    q_ref, k_ref, v_ref, win_ref, w_ref, o_ref,
    listing, qbuf, bias_own, bias, kv, wide, mine, att, near_sum, part_out, part_in, staged,
    send, s_win, r_x, r_plane, r_y, r_q, r_b, r_w, r_att, r_part, r_out,
):
    tile = lax.axis_index("tok")
    p = lax.axis_index("head")
    z = tile // 4
    c = tile % 4
    z_half = z // 2
    z_odd = z % 2
    xn = c + 1 - 2 * (c % 2)
    yn = (c + 2) % 4
    dn = 3 - c
    inner = (c == 1) | (c == 2)
    outer = jnp.logical_not(inner)
    rows = q_ref.shape[0]
    span = q_ref.shape[1] // 2
    heads = span // HD
    quarter = 4 * w_ref.shape[0]
    scale = HD ** (-0.5) * LOG2E

    sent = []

    def remote(src, dst, rsem, zt, ct, ht):
        return pltpu.make_async_remote_copy(
            src_ref=src, dst_ref=dst, send_sem=send.at[len(sent)], recv_sem=rsem,
            device_id=(zt * 4 + ct, ht), device_id_type=MESH,
        )

    def push(src, dst, rsem, zt, ct, ht, when=None):
        copy = remote(src, dst, rsem, zt, ct, ht)
        if when is None:
            copy.start()
        else:
            pl.when(when)(copy.start)
        sent.append((when, copy))

    def put(src, dst, rsem, zt, ct, ht):
        here = (zt == z) & (ht == p)

        @pl.when(here)
        def _():
            pltpu.make_async_copy(src, dst, rsem).start()

        push(src, dst, rsem, zt, ct, ht, jnp.logical_not(here))

    def arrived(dst, rsem):
        pltpu.make_async_copy(dst, dst, rsem).wait()

    def lanes_of(j, base=0):
        return slice(base + j * HD, base + (j + 1) * HD)

    window_copy = pltpu.make_async_copy(win_ref, listing, s_win)
    window_copy.start()
    barrier = pltpu.get_barrier_semaphore()
    for k in range(1, 4):
        for h in range(2):
            pl.semaphore_signal(barrier, inc=1, device_id=((z + k) % 4 * 4 + c, h), device_id_type=MESH)
    for ct in (xn, yn):
        pl.semaphore_signal(barrier, inc=1, device_id=(z * 4 + ct, p), device_id_type=MESH)
    pl.semaphore_signal(barrier, inc=1, device_id=(tile, 1 - p), device_id_type=MESH)

    window_copy.wait()
    row = lax.broadcasted_iota(jnp.int32, (16, win_ref.shape[1]), 0)
    slot = row // 4
    column = jnp.where(slot == 0, c, jnp.where(slot == 1, xn, dn))
    key_tile = row % 4 * 4 + column
    listed = jnp.where(listing[...] == key_tile, 0.0, -1e30)
    bias_own[...] = jnp.broadcast_to(jnp.max(listed, axis=1, keepdims=True), bias_own.shape)

    pl.semaphore_wait(barrier, 9)

    def send_line(j):
        for i in range(2):
            zd = 2 * p + i
            here = lanes_of(j, i * span)
            put(k_ref.at[:, here], kv.at[0, 0, j, z], r_x.at[j, z], zd, c, 0)
            put(v_ref.at[:, here], kv.at[1, 0, j, z], r_x.at[j, z], zd, c, 1)
            put(q_ref.at[:, here], qbuf.at[j, z_odd], r_q.at[j, z_odd], zd, c, z_half)
            if j == 0:
                put(bias_own, bias.at[z_odd], r_b.at[z_odd], zd, c, z_half)

    def share(s, j, when=None):
        push(kv.at[p, s, j], kv.at[p, s, j], r_y.at[s, j], z, c, 1 - p, when)

    def spread_own(j):
        for zz in (z, z + 1 - 2 * z_odd, 2 - z_half, 3 - 3 * z_half):
            piece = kv.at[p, 0, j, zz]
            arrived(piece, r_x.at[j, zz])
            push(piece, kv.at[p, 1, j, zz], r_plane.at[0, j], z, xn, p)
        share(0, j)

    def spread_beside(j):
        piece = kv.at[p, 1, j]
        arrived(piece, r_plane.at[0, j])
        push(piece, kv.at[p, 2, j], r_plane.at[1, j], z, yn, p, outer)
        share(1, j)

    def spread_diagonal(j):
        pl.when(inner)(lambda: arrived(kv.at[p, 2, j], r_plane.at[1, j]))
        share(2, j, inner)

    def attend_slots(j, slots):
        for s in range(slots):
            arrived(kv.at[1 - p, s, j], r_y.at[s, j])
        k_all = kv[0, :slots, j].reshape(slots * 4 * rows, HD)
        v_all = kv[1, :slots, j].reshape(slots * 4 * rows, HD)
        for i in range(2):
            scores = lax.dot_general(
                qbuf[j, i], k_all, (((1,), (1,)), ((), ())), preferred_element_type=jnp.float32
            )
            shift = jnp.concatenate([bias[i, t:t + 1, :] for t in range(slots * 4)], axis=1)
            scores = scores * scale + shift
            peak = jnp.max(scores, axis=1, keepdims=True)
            unrounded = jnp.exp2(scores - peak)
            total = jnp.sum(unrounded, axis=1, keepdims=True)
            summed = jnp.dot(unrounded.astype(jnp.bfloat16), v_all, preferred_element_type=jnp.float32)
            mine[j, i * rows:(i + 1) * rows, :] = (summed / total).astype(jnp.bfloat16)

    def attend(j):
        for i in range(2):
            arrived(qbuf.at[j, i], r_q.at[j, i])
            if j == 0:
                arrived(bias.at[i], r_b.at[i])
        pl.when(inner)(lambda: attend_slots(j, 3))
        pl.when(outer)(lambda: attend_slots(j, 2))
        beyond = jnp.where(z_half == 0, 2, 1)
        for zt in (beyond, z + 1 - 2 * z_odd, z):
            put(mine.at[j], att.at[z_odd, p, j], r_att.at[z_odd, p, j], zt, c, z_half)

    hands_on = ((z == 1) & (p == 1)) | ((z == 2) & (p == 0))
    end = jnp.where(z == 1, 0, 3)

    def hand_on(j):
        for zf in (p, 1 - p):
            for half in range(2):
                piece = att.at[1 - zf, half, j]
                pl.when(hands_on)(lambda: arrived(piece, r_att.at[1 - zf, half, j]))
                push(piece, piece, r_att.at[1 - zf, half, j], end, c, p, hands_on)

    for ct in (xn, yn):
        push(w_ref, wide.at[c], r_w.at[c], z, ct, p)
    pltpu.make_async_copy(w_ref, wide.at[c], r_w.at[c]).start()
    send_line(0)
    send_line(1)
    send_line(2)
    spread_own(0)
    spread_own(1)
    spread_beside(0)
    spread_own(2)
    spread_beside(1)
    spread_diagonal(0)
    attend(0)
    spread_beside(2)
    for ct in (xn, yn):
        arrived(wide.at[ct], r_w.at[ct])
    passed = jnp.where(inner, xn, yn)
    push(wide.at[passed], wide.at[passed], r_w.at[passed], z, jnp.where(inner, yn, xn), p)
    spread_diagonal(1)
    attend(1)
    spread_diagonal(2)
    hand_on(0)
    attend(2)
    hand_on(1)
    hand_on(2)
    arrived(wide.at[c], r_w.at[c])
    arrived(wide.at[dn], r_w.at[dn])

    near = jnp.where(z > 2 * p, 1, 0)

    def features(zf, half):

        @pl.when(jnp.logical_not(hands_on))
        def _():
            for j in range(heads):
                arrived(att.at[zf, half, j], r_att.at[zf, half, j])

        return jnp.concatenate([att[zf, half, j] for j in range(heads)], axis=1)

    def times_weight(attended, zf):
        columns = wide[:, :, pl.ds(pl.multiple_of(zf * span, span), span)].reshape(quarter, span)
        return lax.dot_general(attended, columns, (((1,), (1,)), ((), ())), preferred_element_type=jnp.float32)

    for half in range(2):
        near_sum[half] = times_weight(features(near, half), near)

    def project(half):
        return (near_sum[half] + times_weight(features(1 - near, half), 1 - near)).astype(jnp.bfloat16)

    part_out[...] = project(1 - p)
    push(part_out, part_in, r_part, z, c, 1 - p)
    own = project(p)
    near_sum[p] = own.astype(jnp.float32)
    arrived(part_in, r_part)

    place = pl.ds(pl.multiple_of(z_odd * quarter, quarter), quarter)
    farther = jnp.where(z_half == p, 1 - z_odd, p)
    for i in (farther, 1 - farther):
        mid = pl.ds(pl.multiple_of(i * rows, rows), rows)
        staged[mid, :] = (near_sum[p, mid, :] + part_in[mid, :].astype(jnp.float32)).astype(jnp.bfloat16)
        put(staged.at[mid, :], o_ref.at[:, place], r_out.at[z_odd], 2 * p + i, c, z_half)

    def finish(copies):
        for when, copy in copies:
            if when is None:
                copy.wait_send()
            else:
                pl.when(when)(copy.wait_send)

    finish(sent[:-2])
    for zf in range(2):
        arrived(o_ref.at[:, zf * quarter:(zf + 1) * quarter], r_out.at[zf])
    finish(sent[-2:])


def column_body(queries, keys, values, window, out_weight):
    rows, width = queries.shape
    depth, cols = out_weight.shape
    span = width // 2
    heads = span // HD
    bf16, f32 = jnp.bfloat16, jnp.float32
    dma = pltpu.SemaphoreType.DMA
    hbm = pl.BlockSpec(memory_space=pltpu.HBM)
    copies = heads * (6 + 8 + 3 + 4) + 2 + 3 + 1 + 2
    return pl.pallas_call(
        column_kernel,
        out_shape=jax.ShapeDtypeStruct((rows, 8 * cols), bf16),
        in_specs=[hbm] * 5,
        out_specs=hbm,
        scratch_shapes=[
            pltpu.VMEM((1, window.shape[1]), jnp.int32),
            pltpu.VMEM((heads, 2, rows, HD), bf16),
            pltpu.VMEM((16, 128), f32),
            pltpu.VMEM((2, 16, 128), f32),
            pltpu.VMEM((2, 3, heads, 4, rows, HD), bf16),
            pltpu.VMEM((4, cols, depth), bf16),
            pltpu.VMEM((heads, 2 * rows, HD), bf16),
            pltpu.VMEM((2, 2, heads, 2 * rows, HD), bf16),
            pltpu.VMEM((2, 2 * rows, 4 * cols), f32),
            pltpu.VMEM((2 * rows, 4 * cols), bf16),
            pltpu.VMEM((2 * rows, 4 * cols), bf16),
            pltpu.VMEM((2 * rows, 4 * cols), bf16),
            dma((copies,)), dma,
            dma((heads, 4)), dma((2, heads)), dma((3, heads)), dma((heads, 2)), dma((2,)), dma((4,)), dma((2, 2, heads)), dma, dma((2,)),
        ],
        compiler_params=pltpu.CompilerParams(
            collective_id=0, has_side_effects=True, vmem_limit_bytes=64 * 1024 * 1024 - 65536
        ),
        cost_estimate=pl.CostEstimate(flops=1300000000, bytes_accessed=3000000, transcendentals=1200000),
    )(queries, keys, values, window, out_weight.T)


def solution(mesh):
    in_specs = (
        P("tok", "head"),
        P("tok", "head"),
        P("tok", "head"),
        P("tok", None),
        P("head", "tok"),
    )
    out_specs = P("tok", "head")
    small_grid = mesh.shape["tok"] == 16 and mesh.shape["head"] == 2
    body = column_body if small_grid else general_body
    return jax.shard_map(body, mesh=mesh, in_specs=in_specs, out_specs=out_specs, check_vma=False)
```

```python
import jax
import jax.numpy as jnp
from jax import lax
from jax.experimental import pallas as pl
from jax.experimental.pallas import tpu as pltpu
from jax.sharding import PartitionSpec as P

HD = 128
LOG2E = 1.4426950408889634
MESH = pl.DeviceIdType.MESH


def passed_along(value, axis, by):
    count = lax.axis_size(axis)
    pairs = [(i, i + by) for i in range(count) if 0 <= i + by < count]
    return lax.ppermute(value, axis, pairs)


def attend_tile(running, query_heads, kv_piece, is_listed):
    peak_now, total_now, summed_now = running
    tok_rows, head_count, head_size = query_heads.shape
    key_heads = kv_piece[0].reshape(tok_rows, head_count, head_size)
    value_heads = kv_piece[1].reshape(tok_rows, head_count, head_size)
    scores = jnp.einsum("qhd,khd->hqk", query_heads, key_heads, preferred_element_type=jnp.float32)
    scores = jnp.where(is_listed, scores * HD ** (-0.5), -1e30)
    new_peak = jnp.maximum(peak_now, jnp.max(scores, axis=-1))
    rescale = jnp.exp(peak_now - new_peak)
    unrounded = jnp.exp(scores - new_peak[..., None])
    total_next = total_now * rescale + jnp.sum(unrounded, axis=-1)
    weights = unrounded.astype(jnp.bfloat16)
    summed_next = summed_now * rescale[..., None] + jnp.einsum(
        "hqk,khd->hqd", weights, value_heads, preferred_element_type=jnp.float32
    )
    return (new_peak, total_next, summed_next)


def general_body(queries, keys, values, window, out_weight):
    tok_rows, feat_width = queries.shape
    head_count = feat_width // HD
    tile_count = lax.axis_size("tok")
    grid_w = min(8, tile_count // 4)
    grid_h = min(4, tile_count // (2 * grid_w))
    frame_size = grid_w * grid_h
    frame_count = tile_count // frame_size
    my_tile = lax.axis_index("tok")
    my_frame = my_tile // frame_size
    my_row = my_tile // grid_w % grid_h
    my_col = my_tile % grid_w
    query_heads = queries.reshape(tok_rows, head_count, HD)
    listed_tiles = window[0]
    initial = (
        jnp.full((head_count, tok_rows), -1e30, jnp.float32),
        jnp.zeros((head_count, tok_rows), jnp.float32),
        jnp.zeros((head_count, tok_rows, HD), jnp.float32),
    )
    own_pair = jnp.stack([keys, values])
    slot_blocks = []
    for step_f in (-1, 0, 1):
        for step_h in (-1, 0, 1):
            for step_w in (-1, 0, 1):
                distance = step_f * frame_size + step_h * grid_w + step_w
                if distance == 0:
                    slot_blocks.append(own_pair)
                else:
                    slot_blocks.append(passed_along(own_pair, "tok", -distance))
    near_box = jnp.stack(slot_blocks)
    slot_range = jnp.arange(27, dtype=jnp.int32)
    slot_f = slot_range // 9 - 1
    slot_h = slot_range // 3 % 3 - 1
    slot_w = slot_range % 3 - 1
    slot_distance = slot_f * frame_size + slot_h * grid_w + slot_w
    inside = (
        (my_frame + slot_f >= 0)
        & (my_frame + slot_f < frame_count)
        & (my_row + slot_h >= 0)
        & (my_row + slot_h < grid_h)
        & (my_col + slot_w >= 0)
        & (my_col + slot_w < grid_w)
    )

    def visit_band(running, slot_index):
        key_tile = my_tile + slot_distance[slot_index]
        is_listed = inside[slot_index] & jnp.any(listed_tiles == key_tile)
        kv_piece = lax.dynamic_index_in_dim(near_box, slot_index, 0, keepdims=False)
        return (attend_tile(running, query_heads, kv_piece, is_listed), None)

    running, _ = lax.scan(visit_band, initial, slot_range)
    attended = (running[2] / running[1][..., None]).transpose(1, 0, 2).reshape(tok_rows, feat_width)
    attended = attended.astype(jnp.bfloat16)
    projection = jnp.dot(
        attended,
        lax.all_gather(out_weight, "tok", axis=1, tiled=True),
        preferred_element_type=jnp.float32,
    )
    return lax.psum_scatter(
        projection.astype(jnp.bfloat16), "head", scatter_dimension=1, tiled=True
    )


def column_kernel(
    q_ref, k_ref, v_ref, win_ref, w_ref, o_ref,
    listing, qbuf, bias_own, bias, kv, wide, mine, att, near_sum, part_out, part_in, staged,
    send, s_win, r_x, r_plane, r_y, r_q, r_b, r_w, r_att, r_part, r_out,
):
    tile = lax.axis_index("tok")
    p = lax.axis_index("head")
    z = tile // 4
    c = tile % 4
    z_half = z // 2
    z_odd = z % 2
    xn = c + 1 - 2 * (c % 2)
    yn = (c + 2) % 4
    dn = 3 - c
    inner = (c == 1) | (c == 2)
    outer = jnp.logical_not(inner)
    rows = q_ref.shape[0]
    span = q_ref.shape[1] // 2
    heads = span // HD
    quarter = 4 * w_ref.shape[0]
    scale = HD ** (-0.5) * LOG2E

    sent = []

    def remote(src, dst, rsem, zt, ct, ht):
        return pltpu.make_async_remote_copy(
            src_ref=src, dst_ref=dst, send_sem=send.at[len(sent)], recv_sem=rsem,
            device_id=(zt * 4 + ct, ht), device_id_type=MESH,
        )

    def push(src, dst, rsem, zt, ct, ht, when=None):
        copy = remote(src, dst, rsem, zt, ct, ht)
        if when is None:
            copy.start()
        else:
            pl.when(when)(copy.start)
        sent.append((when, copy))

    def put(src, dst, rsem, zt, ct, ht):
        here = (zt == z) & (ht == p)

        @pl.when(here)
        def _():
            pltpu.make_async_copy(src, dst, rsem).start()

        push(src, dst, rsem, zt, ct, ht, jnp.logical_not(here))

    def arrived(dst, rsem):
        pltpu.make_async_copy(dst, dst, rsem).wait()

    def lanes_of(j, base=0):
        return slice(base + j * HD, base + (j + 1) * HD)

    window_copy = pltpu.make_async_copy(win_ref, listing, s_win)
    window_copy.start()
    barrier = pltpu.get_barrier_semaphore()
    for k in range(1, 4):
        for h in range(2):
            pl.semaphore_signal(barrier, inc=1, device_id=((z + k) % 4 * 4 + c, h), device_id_type=MESH)
    for ct in (xn, yn):
        pl.semaphore_signal(barrier, inc=1, device_id=(z * 4 + ct, p), device_id_type=MESH)
    pl.semaphore_signal(barrier, inc=1, device_id=(tile, 1 - p), device_id_type=MESH)

    window_copy.wait()
    row = lax.broadcasted_iota(jnp.int32, (16, win_ref.shape[1]), 0)
    slot = row // 4
    column = jnp.where(slot == 0, c, jnp.where(slot == 1, xn, dn))
    key_tile = row % 4 * 4 + column
    listed = jnp.where(listing[...] == key_tile, 0.0, -1e30)
    bias_own[...] = jnp.broadcast_to(jnp.max(listed, axis=1, keepdims=True), bias_own.shape)

    pl.semaphore_wait(barrier, 9)

    def send_line(j):
        for i in range(2):
            zd = 2 * p + i
            here = lanes_of(j, i * span)
            put(k_ref.at[:, here], kv.at[0, 0, j, z], r_x.at[j, z], zd, c, 0)
            put(v_ref.at[:, here], kv.at[1, 0, j, z], r_x.at[j, z], zd, c, 1)
            put(q_ref.at[:, here], qbuf.at[j, z_odd], r_q.at[j, z_odd], zd, c, z_half)
            if j == 0:
                put(bias_own, bias.at[z_odd], r_b.at[z_odd], zd, c, z_half)

    def share(s, j, when=None):
        push(kv.at[p, s, j], kv.at[p, s, j], r_y.at[s, j], z, c, 1 - p, when)

    def spread_own(j):
        for zz in (z, z + 1 - 2 * z_odd, 2 - z_half, 3 - 3 * z_half):
            piece = kv.at[p, 0, j, zz]
            arrived(piece, r_x.at[j, zz])
            push(piece, kv.at[p, 1, j, zz], r_plane.at[0, j], z, xn, p)
        share(0, j)

    def spread_beside(j):
        piece = kv.at[p, 1, j]
        arrived(piece, r_plane.at[0, j])
        push(piece, kv.at[p, 2, j], r_plane.at[1, j], z, yn, p, outer)
        share(1, j)

    def spread_diagonal(j):
        pl.when(inner)(lambda: arrived(kv.at[p, 2, j], r_plane.at[1, j]))
        share(2, j, inner)

    def attend_slots(j, slots):
        for s in range(slots):
            arrived(kv.at[1 - p, s, j], r_y.at[s, j])
        k_all = kv[0, :slots, j].reshape(slots * 4 * rows, HD)
        v_all = kv[1, :slots, j].reshape(slots * 4 * rows, HD)
        for i in range(2):
            scores = lax.dot_general(
                qbuf[j, i], k_all, (((1,), (1,)), ((), ())), preferred_element_type=jnp.float32
            )
            shift = jnp.concatenate([bias[i, t:t + 1, :] for t in range(slots * 4)], axis=1)
            scores = scores * scale + shift
            peak = jnp.max(scores, axis=1, keepdims=True)
            unrounded = jnp.exp2(scores - peak)
            total = jnp.sum(unrounded, axis=1, keepdims=True)
            summed = jnp.dot(unrounded.astype(jnp.bfloat16), v_all, preferred_element_type=jnp.float32)
            mine[j, i * rows:(i + 1) * rows, :] = (summed / total).astype(jnp.bfloat16)

    def attend(j):
        for i in range(2):
            arrived(qbuf.at[j, i], r_q.at[j, i])
            if j == 0:
                arrived(bias.at[i], r_b.at[i])
        pl.when(inner)(lambda: attend_slots(j, 3))
        pl.when(outer)(lambda: attend_slots(j, 2))
        beyond = jnp.where(z_half == 0, 2, 1)
        for zt in (beyond, z + 1 - 2 * z_odd, z):
            put(mine.at[j], att.at[z_odd, p, j], r_att.at[z_odd, p, j], zt, c, z_half)

    hands_on = ((z == 1) & (p == 1)) | ((z == 2) & (p == 0))
    end = jnp.where(z == 1, 0, 3)

    def hand_on(j):
        for zf in (p, 1 - p):
            for half in range(2):
                piece = att.at[1 - zf, half, j]
                pl.when(hands_on)(lambda: arrived(piece, r_att.at[1 - zf, half, j]))
                push(piece, piece, r_att.at[1 - zf, half, j], end, c, p, hands_on)

    for ct in (xn, yn):
        push(w_ref, wide.at[c], r_w.at[c], z, ct, p)
    pltpu.make_async_copy(w_ref, wide.at[c], r_w.at[c]).start()
    send_line(0)
    send_line(1)
    spread_own(0)
    send_line(2)
    spread_own(1)
    spread_beside(0)
    spread_own(2)
    spread_beside(1)
    spread_diagonal(0)
    attend(0)
    spread_beside(2)
    for ct in (xn, yn):
        arrived(wide.at[ct], r_w.at[ct])
    passed = jnp.where(inner, xn, yn)
    push(wide.at[passed], wide.at[passed], r_w.at[passed], z, jnp.where(inner, yn, xn), p)
    spread_diagonal(1)
    attend(1)
    spread_diagonal(2)
    hand_on(0)
    attend(2)
    hand_on(1)
    hand_on(2)
    arrived(wide.at[c], r_w.at[c])
    arrived(wide.at[dn], r_w.at[dn])

    near = jnp.where(z > 2 * p, 1, 0)

    def features(zf, half):

        @pl.when(jnp.logical_not(hands_on))
        def _():
            for j in range(heads):
                arrived(att.at[zf, half, j], r_att.at[zf, half, j])

        return jnp.concatenate([att[zf, half, j] for j in range(heads)], axis=1)

    def times_weight(attended, zf):
        columns = wide[:, :, pl.ds(pl.multiple_of(zf * span, span), span)].reshape(quarter, span)
        return lax.dot_general(attended, columns, (((1,), (1,)), ((), ())), preferred_element_type=jnp.float32)

    for half in range(2):
        near_sum[half] = times_weight(features(near, half), near)

    def project(half):
        return (near_sum[half] + times_weight(features(1 - near, half), 1 - near)).astype(jnp.bfloat16)

    part_out[...] = project(1 - p)
    push(part_out, part_in, r_part, z, c, 1 - p)
    own = project(p).astype(jnp.float32)
    arrived(part_in, r_part)

    place = pl.ds(pl.multiple_of(z_odd * quarter, quarter), quarter)
    for i in range(2):
        mid = slice(i * rows, (i + 1) * rows)
        staged[mid, :] = (own[mid, :] + part_in[mid, :].astype(jnp.float32)).astype(jnp.bfloat16)
        put(staged.at[mid, :], o_ref.at[:, place], r_out.at[z_odd], 2 * p + i, c, z_half)
    for zf in range(2):
        arrived(o_ref.at[:, zf * quarter:(zf + 1) * quarter], r_out.at[zf])

    for when, copy in sent:
        if when is None:
            copy.wait_send()
        else:
            pl.when(when)(copy.wait_send)


def column_body(queries, keys, values, window, out_weight):
    rows, width = queries.shape
    depth, cols = out_weight.shape
    span = width // 2
    heads = span // HD
    bf16, f32 = jnp.bfloat16, jnp.float32
    dma = pltpu.SemaphoreType.DMA
    hbm = pl.BlockSpec(memory_space=pltpu.HBM)
    copies = heads * (6 + 8 + 3 + 4) + 2 + 3 + 1 + 2
    return pl.pallas_call(
        column_kernel,
        out_shape=jax.ShapeDtypeStruct((rows, 8 * cols), bf16),
        in_specs=[hbm] * 5,
        out_specs=hbm,
        scratch_shapes=[
            pltpu.VMEM((1, window.shape[1]), jnp.int32),
            pltpu.VMEM((heads, 2, rows, HD), bf16),
            pltpu.VMEM((16, 128), f32),
            pltpu.VMEM((2, 16, 128), f32),
            pltpu.VMEM((2, 3, heads, 4, rows, HD), bf16),
            pltpu.VMEM((4, cols, depth), bf16),
            pltpu.VMEM((heads, 2 * rows, HD), bf16),
            pltpu.VMEM((2, 2, heads, 2 * rows, HD), bf16),
            pltpu.VMEM((2, 2 * rows, 4 * cols), f32),
            pltpu.VMEM((2 * rows, 4 * cols), bf16),
            pltpu.VMEM((2 * rows, 4 * cols), bf16),
            pltpu.VMEM((2 * rows, 4 * cols), bf16),
            dma((copies,)), dma,
            dma((heads, 4)), dma((2, heads)), dma((3, heads)), dma((heads, 2)), dma((2,)), dma((4,)), dma((2, 2, heads)), dma, dma((2,)),
        ],
        compiler_params=pltpu.CompilerParams(
            collective_id=0, has_side_effects=True, vmem_limit_bytes=64 * 1024 * 1024 - 65536
        ),
        cost_estimate=pl.CostEstimate(flops=1300000000, bytes_accessed=3000000, transcendentals=1200000),
    )(queries, keys, values, window, out_weight.T)


def solution(mesh):
    in_specs = (
        P("tok", "head"),
        P("tok", "head"),
        P("tok", "head"),
        P("tok", None),
        P("head", "tok"),
    )
    out_specs = P("tok", "head")
    small_grid = mesh.shape["tok"] == 16 and mesh.shape["head"] == 2
    body = column_body if small_grid else general_body
    return jax.shard_map(body, mesh=mesh, in_specs=in_specs, out_specs=out_specs, check_vma=False)
```
